128 devices in a mesh: gx: 16 (over x, z), gy: 8 (over y, core).
Axes of the slice: x: 4, y: 4, z: 4, core: 2. Of those that a mesh axis runs over, the one named last changes fastest.
Arguments:
- positions: float32 [3, 2048, 256], P(None, ('gx', 'gy')), may hold values from 0 to 1
- velocities: float32 [3, 2048, 256], P(None, ('gx', 'gy')), may hold values from -6 to 6
- masses: float32 [2048, 256], P(('gx', 'gy')), may hold values from 0.004 to 0.016
- smoothing: float32 [2048, 256], P(('gx', 'gy')), may hold values from 0.35 to 0.6
- sound2: float32 [2048, 256], P(('gx', 'gy')), may hold values from 0.5 to 2
- counts: int32 [2048], P(('gx', 'gy')), may hold values from 64 to 256, as said below
- move_to: int32 [2048], P(('gx', 'gy')), may hold values from 0 to 2047, as said below
- proxy_send: int32 [16384], P(('gx', 'gy')), may hold values from 0 to 15
- pairs: int32 [20480, 3], P(('gx', 'gy')), may hold values from 0 to 143, as said below
Outputs:
- density: float32 [2048, 256], P(('gx', 'gy'))
- accel: float32 [3, 2048, 256], P(None, ('gx', 'gy'))
The draws below stay inside these ranges and needn't reach their ends.
Inputs may be any that keep to these rules, and one draw needn't show every extreme that they name: `counts`: every cell holds at least 64 particles; some cell in every draw holds 256. move_to is a permutation; every cell stays on the same index of gy; one device hands at most 2 cells to any one device, and exactly 2 to each device it sends to. `pairs`: own cell numbers are below 16, source cells index the device's cell list (below 144), directions run from 0 to 26 with 13 the zero offset; each own cell has its zero-offset self pair and each proxy cell appears in exactly one pair.
All inputs are finite; a program needn't handle non-finite values.
Results may differ from the reference program's by a relative error of at most 0.0003.
Values sent between devices are 32-bit elements; how exact they have to be, the bound alone decides.
A program may use at most 64 MiB of HBM per device.

```python
import math
import jax
import jax.numpy as jnp
import numpy as np
from jax import lax

P_SIZE = 256
CELLS_DEV = 16
PCAP = 16
CAP = 2
NCELL = 2048
PAIRS_DEV = 160
N_GX = 16
N_GY = 8


def draw_move_to(key, part):
    key = jax.random.fold_in(key, 5)
    rows = jnp.arange(N_GY)

    def shuffle_columns(row):
        return jax.random.permutation(jax.random.fold_in(key, 100 + row), N_GX)

    def shuffle_order(row):
        return jax.random.permutation(jax.random.fold_in(key, 200 + row), CELLS_DEV)

    def shuffle_slots(row):
        return jax.random.permutation(jax.random.fold_in(key, 300 + row), CELLS_DEV)
    shifts = jax.vmap(shuffle_columns)(rows)
    orders = jax.vmap(shuffle_order)(rows)
    targets = jax.vmap(shuffle_slots)(rows)
    column = jnp.arange(N_GX)[:, None, None]
    row_index = jnp.arange(N_GY)[None, :, None]
    local = jnp.arange(CELLS_DEV)[None, None, :]
    sigma = orders[row_index, local]
    shift = shifts[row_index, sigma // CAP]
    dest_col = (column + shift) % N_GX
    slot = targets[row_index, sigma]
    return ((dest_col * N_GY + row_index) * CELLS_DEV + slot).reshape(-1).astype(jnp.int32)


def draw_counts(key, part):
    key = jax.random.fold_in(key, 7)
    base = jax.random.randint(key, (NCELL,), P_SIZE // 4, P_SIZE + 1)
    chosen = jax.random.randint(jax.random.fold_in(key, 1), (), 0, NCELL)
    return jnp.where(jnp.arange(NCELL) == chosen, P_SIZE, base).astype(jnp.int32)


def draw_pairs(key, part):
    key = jax.random.fold_in(key, 11)
    proxy_total = 8 * PCAP

    def one_device(device):
        sub = jax.random.fold_in(key, device)
        own = jnp.arange(CELLS_DEV)
        self_rows = jnp.stack([own, own, jnp.full((CELLS_DEV,), 13)], 1)
        receivers = jax.random.randint(jax.random.fold_in(sub, 1), (proxy_total,), 0, CELLS_DEV)
        proxy_dirs = jax.random.randint(jax.random.fold_in(sub, 2), (proxy_total,), 0, 27)
        proxy_rows = jnp.stack([receivers, CELLS_DEV + jnp.arange(proxy_total), proxy_dirs], 1)
        extra_dirs = jax.random.randint(jax.random.fold_in(sub, 3), (CELLS_DEV,), 0, 26)
        extra_dirs = extra_dirs + (extra_dirs >= 13).astype(jnp.int32)
        partners = jax.random.randint(jax.random.fold_in(sub, 4), (CELLS_DEV,), 0, CELLS_DEV)
        extra_rows = jnp.stack([own, partners, extra_dirs], 1)
        joined = jnp.concatenate([self_rows, proxy_rows, extra_rows], 0)
        shuffled = jax.random.permutation(jax.random.fold_in(sub, 5), PAIRS_DEV)
        return joined[shuffled]
    table = jax.vmap(one_device)(jnp.arange(N_GX * N_GY))
    return table.reshape(-1, 3).astype(jnp.int32)


def plant(result, own_key, least, largest):
    dims = result.shape
    index_at = [jax.random.randint(jax.random.fold_in(own_key, axis), (), 0, dims[axis]) for axis in range(len(dims))]
    result = result.at[tuple(index_at)].set(least)
    longest = dims.index(max(dims))
    index_at[longest] = (index_at[longest] + 1) % dims[longest]
    return result.at[tuple(index_at)].set(largest)


def level_of(own_key, dims, shards, smallest, top_value):
    def one(position, shards_of):
        draws = jax.random.uniform(jax.random.fold_in(jax.random.fold_in(own_key, 6), position), (shards_of,), jnp.float32, smallest / len(shards), top_value / len(shards))
        return jnp.repeat(jnp.exp(draws), dims[position] // shards_of).reshape((-1,) + (1,) * (len(dims) - position - 1))

    level = one(*shards[0])
    for cut in shards[1:]:
        level = level * one(*cut)
    return level


def normal_values(key, shape, scale, reach, cuts=(), kind=jnp.bfloat16):
    result = scale * jax.random.normal(key, shape, jnp.float32)
    if cuts:
        result = result * level_of(key, shape, cuts, -0.22, 0.18)
    return jnp.clip(result, -reach, reach).astype(kind)


def setup_inputs(seed: int = 0) -> dict:
    seeds = jax.random.split(jax.random.key(seed), 10)
    return {
        "positions": jnp.clip(1.0 * jax.random.uniform(seeds[0], (3, NCELL, P_SIZE), jnp.float32) ** level_of(seeds[0], (3, NCELL, P_SIZE), ((1, 128),), -0.2, 0.2), 0.0, 1.0),
        "velocities": normal_values(seeds[1], (3, NCELL, P_SIZE), 1.0, 6.0, ((1, 128),), jnp.float32),
        "masses": jnp.clip(jnp.exp(math.log(0.016) - 1.3862944 * jax.random.uniform(seeds[2], (NCELL, P_SIZE), jnp.float32) ** level_of(seeds[2], (NCELL, P_SIZE), ((0, 128),), -0.2, 0.2)), 0.004, 0.016),
        "smoothing": jnp.clip(0.35 + 0.25000003 * jax.random.uniform(seeds[3], (NCELL, P_SIZE), jnp.float32) ** level_of(seeds[3], (NCELL, P_SIZE), ((0, 128),), -0.2, 0.2), 0.35, 0.6),
        "sound2": jnp.clip(jnp.exp(math.log(2.0) - 1.3862944 * jax.random.uniform(seeds[4], (NCELL, P_SIZE), jnp.float32) ** level_of(seeds[4], (NCELL, P_SIZE), ((0, 128),), -0.2, 0.2)), 0.5, 2.0),
        "counts": draw_counts(jax.random.fold_in(seeds[9], 71), 0),
        "move_to": draw_move_to(jax.random.fold_in(seeds[9], 71), 0),
        "proxy_send": plant(jax.random.randint(seeds[7], (N_GX * N_GY * 8 * PCAP,), 0, CELLS_DEV), jax.random.fold_in(seeds[7], 1), 0, CELLS_DEV - 1).astype(jnp.int32),
        "pairs": draw_pairs(jax.random.fold_in(seeds[9], 71), 0),
    }


KERNEL_NORM = 21.0 / (16.0 * math.pi)
VISC_ALPHA = 1.0
VISC_BETA = 2.0
BLOCK_PAIRS = 8
HIGHEST = lax.Precision.HIGHEST
NEIGHBOUR_DX = np.array([-1, -1, -1, 0, 0, 1, 1, 1], dtype=np.int32)
NEIGHBOUR_DY = np.array([-1, 0, 1, -1, 1, -1, 0, 1], dtype=np.int32)

def cell_offsets(direction):
    return jnp.stack([direction // 9 - 1, direction // 3 % 3 - 1, direction % 3 - 1]).astype(jnp.float32)

def pair_geometry(block, ipos, jpos, ismooth, jsmooth):
    target = block[:, 0]
    source = block[:, 1]
    shifted = jnp.take(jpos, source, axis=1) + cell_offsets(block[:, 2])[:, :, None]
    here = jnp.take(ipos, target, axis=1)
    separation = here[:, :, :, None] - shifted[:, :, None, :]
    radius2 = lax.optimization_barrier(jnp.sum(separation * separation, axis=0))
    length = 0.5 * (jnp.take(ismooth, target, axis=0)[:, :, None] + jnp.take(jsmooth, source, axis=0)[:, None, :])
    ratio = jnp.sqrt(radius2) / length
    falloff = jnp.maximum(1.0 - 0.5 * ratio, 0.0)
    return (target, source, separation, radius2, length, ratio, falloff)

def density_sum(pair_list, cell_count, ipos, ismooth, jpos, jmass, jsmooth):
    blocks = pair_list.reshape(-1, BLOCK_PAIRS, 3)

    def step(total, block):
        target, source, separation, radius2, length, ratio, falloff = pair_geometry(block, ipos, jpos, ismooth, jsmooth)
        kernel = KERNEL_NORM / length ** 3 * falloff ** 4 * (1.0 + 2.0 * ratio)
        contrib = lax.optimization_barrier(jnp.sum(jnp.take(jmass, source, axis=0)[:, None, :] * kernel, axis=2))
        onehot = (target[:, None] == jnp.arange(cell_count, dtype=jnp.int32)[None, :]).astype(jnp.float32)
        return (total + jnp.einsum('bc,bp->cp', onehot, contrib, precision=HIGHEST), None)
    start = jnp.zeros((cell_count, ipos.shape[2]), jnp.float32)
    return lax.scan(step, start, blocks)[0]

def force_sum(pair_list, cell_count, ipos, ivel, ismooth, isound, irho, jpos, jvel, jmass, jsmooth, jsound, jrho):
    blocks = pair_list.reshape(-1, BLOCK_PAIRS, 3)

    def step(total, block):
        target, source, separation, radius2, length, ratio, falloff = pair_geometry(block, ipos, jpos, ismooth, jsmooth)
        gradient = -5.0 * KERNEL_NORM / length ** 5 * falloff ** 3
        relvel = jnp.take(ivel, target, axis=1)[:, :, :, None] - jnp.take(jvel, source, axis=1)[:, :, None, :]
        approach = jnp.minimum(lax.optimization_barrier(jnp.sum(relvel * separation, axis=0)), 0.0)
        compress = length * approach / (radius2 + 0.01 * length * length)
        sound_i = jnp.take(isound, target, axis=0)[:, :, None]
        sound_j = jnp.take(jsound, source, axis=0)[:, None, :]
        rho_i = jnp.take(irho, target, axis=0)[:, :, None]
        rho_j = jnp.take(jrho, source, axis=0)[:, None, :]
        speed = 0.5 * (jnp.sqrt(sound_i) + jnp.sqrt(sound_j))
        viscous = (-VISC_ALPHA * speed * compress + VISC_BETA * compress * compress) / (0.5 * (rho_i + rho_j))
        factor = jnp.take(jmass, source, axis=0)[:, None, :] * (sound_i / rho_i + sound_j / rho_j + viscous) * gradient
        contrib = -lax.optimization_barrier(jnp.sum(factor[None] * separation, axis=3))
        onehot = (target[:, None] == jnp.arange(cell_count, dtype=jnp.int32)[None, :]).astype(jnp.float32)
        return (total + jnp.einsum('bc,xbp->xcp', onehot, contrib, precision=HIGHEST), None)
    start = jnp.zeros((3, cell_count, ipos.shape[2]), jnp.float32)
    return lax.scan(step, start, blocks)[0]

def proxy_cells(proxy_send):
    device_count = N_GX * N_GY
    devices = jnp.arange(device_count, dtype=jnp.int32)
    column = devices // N_GY
    row_index = devices % N_GY
    step_x = jnp.asarray(NEIGHBOUR_DX, dtype=jnp.int32)
    step_y = jnp.asarray(NEIGHBOUR_DY, dtype=jnp.int32)
    sender = ((column[:, None] - step_x[None, :]) % N_GX * N_GY + (row_index[:, None] - step_y[None, :]) % N_GY).astype(jnp.int32)
    sends = proxy_send.reshape(device_count, 8, PCAP)
    picked = sends[sender, jnp.arange(8, dtype=jnp.int32)[None, :]]
    cells = sender[:, :, None] * CELLS_DEV + picked
    return cells.reshape(device_count, 8 * PCAP).astype(jnp.int32)

def reference(positions, velocities, masses, smoothing, sound2, counts, move_to, proxy_send, pairs):
    device_count = N_GX * N_GY
    occupied = (lax.broadcasted_iota(jnp.int32, (NCELL, P_SIZE), 1) < counts[:, None]).astype(jnp.float32)
    record = jnp.concatenate([positions, velocities, (masses * occupied)[None], smoothing[None], sound2[None], occupied[None]], 0)
    moved = jnp.zeros_like(record).at[:, move_to, :].set(record)
    proxy_table = proxy_cells(proxy_send)
    pair_table = pairs.reshape(device_count, PAIRS_DEV, 3)

    def gather_cells(field, device):
        local = lax.dynamic_slice_in_dim(field, (device * CELLS_DEV).astype(jnp.int32), CELLS_DEV, axis=field.ndim - 2)
        remote = jnp.take(field, proxy_table[device], axis=field.ndim - 2)
        return (local, jnp.concatenate([local, remote], axis=field.ndim - 2))

    def density_device(device):
        local, joined = gather_cells(moved, device)
        return density_sum(pair_table[device], CELLS_DEV, local[0:3], local[7], joined[0:3], joined[6], joined[7])
    rho = lax.map(density_device, jnp.arange(device_count, dtype=jnp.int32)).reshape(NCELL, P_SIZE)
    filled = moved[9]
    safe_rho = jnp.where(filled > 0, rho, 1.0)

    def force_device(device):
        local, joined = gather_cells(moved, device)
        local_rho, joined_rho = gather_cells(safe_rho, device)
        return force_sum(pair_table[device], CELLS_DEV, local[0:3], local[3:6], local[7], local[8], local_rho, joined[0:3], joined[3:6], joined[6], joined[7], joined[8], joined_rho)
    forces = lax.map(force_device, jnp.arange(device_count, dtype=jnp.int32))
    accel = forces.transpose(1, 0, 2, 3).reshape(3, NCELL, P_SIZE)
    return (rho * filled, accel * filled[None])
```

```python
import math, functools
import jax, jax.numpy as jnp
from jax import lax
from jax.experimental import pallas as pl
from jax.experimental.pallas import tpu as pltpu

CELLS=16; SLOTS=256; NPAIRS=160; NORM=21.0/(16.0*math.pi)
MAXT=2*NPAIRS+CELLS+8
FIRST=2*NPAIRS

def rcp(x, approx=True):
    return pl.reciprocal(x, approx=approx)

def append(buf, x0, x1, pos, lane):
    tile=lax.shift_right_logical(pos,7); s=lax.bitwise_and(pos,127)
    t0=pltpu.roll(x0,s,1); t1=pltpu.roll(x1,s,1)
    keep=lane>=s
    buf[tile]=jnp.where(keep,t0,buf[tile])
    buf[tile+1]=jnp.where(keep,t1,t0)
    buf[tile+2]=jnp.where(keep,0.0,t1)

def plan(meta, pairs, tab, head, link):
    for a in range(CELLS):
        head[a]=-1
    def chain(p,_):
        a=pairs[3*p]
        link[p]=head[a]
        head[a]=p
        return 0
    lax.fori_loop(0,NPAIRS,chain,0)

def pack_main(rec, meta, pairs, tab, head, link, buf):
    lane=lax.broadcasted_iota(jnp.int32,(8,128),1)
    row=lax.broadcasted_iota(jnp.int32,(8,128),0)
    def cell(a,carry):
        k,tile=carry
        tab[FIRST+a]=tile
        def cond(c): return c[0]>=0
        def step(c):
            p,k,pos=c
            b=pairs[3*p+1]; d=pairs[3*p+2]
            n=lax.shift_right_logical(b,4)
            r=lax.bitwise_and(b,15)
            cell_=jnp.where(n==0,r,meta[n*128+16+r])
            src=n*16+cell_
            count=meta[n*128+cell_]
            tab[k]=src; tab[NPAIRS+k]=pos
            dx=d//9; dy=d//3-3*dx; dz=d-3*(d//3)
            shift=jnp.where(row==0,dx,jnp.where(row==1,dy,dz))-1
            shift=jnp.where(row<3,shift,0).astype(jnp.float32)
            append(buf,rec[src,:,0:128]+shift,rec[src,:,128:256]+shift,pos,lane)
            return link[p],k+1,pos+count
        _,k,pos=lax.while_loop(cond,step,(head[a],k,tile*128))
        return k,lax.shift_right_logical(pos+127,7)
    _,tile=lax.fori_loop(0,CELLS,cell,(0,0))
    tab[FIRST+CELLS]=tile

def spread(dst, f, rows):
    dst[f]=jnp.broadcast_to(rows.T,(SLOTS,128))

def density_kernel(IB,JB,approx,rec,meta,pairs,rho,safe,tab,buf,head,link,icol,acc):
    plan(meta,pairs,tab,head,link)
    pack_main(rec,meta,pairs,tab,head,link,buf)
    def cell(a,_):
        cols=rec[a].T
        for f,rw in enumerate((0,1,2,4)):
            icol[f]=jnp.broadcast_to(cols[:,rw:rw+1],(SLOTS,128))
        first=tab[FIRST+a]; last=tab[FIRST+a+1]
        nfull=(last-first)//JB
        count=meta[a]
        def iblock(g,_):
            rows=pl.ds(pl.multiple_of(g*IB,IB),IB)
            xi,yi,zi,hi=(icol[f,rows,:] for f in range(4))
            def tile(t):
                j=lambda rw: buf[t,rw:rw+1,:]
                dx=xi-j(0); dy=yi-j(1); dz=zi-j(2)
                r2=dx*dx+dy*dy+dz*dz
                s=hi+j(4)
                inv=rcp(s,approx)
                r=r2*lax.rsqrt(jnp.maximum(r2,1e-30))
                w=jnp.maximum(inv-r*(inv*inv),0.0)
                t_=w*s
                return (w*w)*(w*t_)*((1.25-t_)*j(3))
            def many(k,total):
                t=first+k*JB
                return total+functools.reduce(lambda p,q:p+q,[tile(t+i) for i in range(JB)])
            total=lax.fori_loop(0,nfull,many,jnp.zeros((IB,128),jnp.float32))
            if JB>1:
                total=lax.fori_loop(first+nfull*JB,last,lambda t,tt:tt+tile(t),total)
            acc[a,rows,:]=total
            return 0
        lax.fori_loop(0,(count+IB-1)//IB,iblock,0)
        return 0
    lax.fori_loop(0,CELLS,cell,0)
    for a in range(CELLS):
        sums=jnp.sum(acc[a].T,axis=0,keepdims=True)
        there=rec[a,3:4,:]>0
        rho[a:a+1,:]=jnp.where(there,(32.0*NORM)*sums,0.0)
        safe[a:a+1,:]=jnp.where(there,(32.0*NORM)*sums,1.0)

def density(rec,meta,pairs,IB=64,JB=2,approx=True):
    V=pl.BlockSpec(memory_space=pltpu.VMEM); S=pl.BlockSpec(memory_space=pltpu.SMEM)
    return pl.pallas_call(functools.partial(density_kernel,IB,JB,approx),
        out_shape=(jax.ShapeDtypeStruct((CELLS,SLOTS),jnp.float32),jax.ShapeDtypeStruct((CELLS,SLOTS),jnp.float32),jax.ShapeDtypeStruct((384,),jnp.int32),jax.ShapeDtypeStruct((MAXT,8,128),jnp.float32)),
        in_specs=[V,S,S],out_specs=(V,V,S,V),
        scratch_shapes=[pltpu.SMEM((CELLS,),jnp.int32),pltpu.SMEM((NPAIRS,),jnp.int32),pltpu.VMEM((4,SLOTS,128),jnp.float32),pltpu.VMEM((CELLS,SLOTS,128),jnp.float32)],
        compiler_params=pltpu.CompilerParams(vmem_limit_bytes=48<<20),
        name="density")(rec,meta,pairs)

def force_kernel(IB,JB,approx,rec,snd,rho,meta,tab,buf,out,extra,cells,icol,acc):
    for n in range(9):
        for half in range(2):
            c8=slice(8*half,8*half+8)
            c2=snd[n,c8,:]; rr=rho[n,c8,:]
            base=(n*16+8*half)*8
            for c in range(8):
                cells[n*16+8*half+c,0:1,:]=0.5*jnp.sqrt(c2[c:c+1])
                cells[n*16+8*half+c,1:2,:]=c2[c:c+1]/rr[c:c+1]
                cells[n*16+8*half+c,2:3,:]=rr[c:c+1]
    lane=lax.broadcasted_iota(jnp.int32,(8,128),1)
    def put(k,_):
        src=tab[k]
        append(extra,cells[src,:,0:128],cells[src,:,128:256],tab[NPAIRS+k],lane)
        return 0
    lax.fori_loop(0,NPAIRS,put,0,unroll=2)
    def cell(a,_):
        cols=rec[a].T; more=cells[a].T
        for f,rw in enumerate((0,1,2,4,5,6,7)):
            icol[f]=jnp.broadcast_to(cols[:,rw:rw+1],(SLOTS,128))
        for f in range(3):
            icol[7+f]=jnp.broadcast_to(more[:,f:f+1],(SLOTS,128))
        first=tab[FIRST+a]; last=tab[FIRST+a+1]
        nfull=(last-first)//JB
        count=meta[a]
        def iblock(g,_):
            rows=pl.ds(pl.multiple_of(g*IB,IB),IB)
            def tile(t):
                i=lambda f: icol[f,rows,:]
                j=lambda rw: buf[t,rw:rw+1,:]
                e=lambda rw: extra[t,rw:rw+1,:]
                dx=i(0)-j(0); dy=i(1)-j(1); dz=i(2)-j(2)
                r2=dx*dx+dy*dy+dz*dz
                s=i(3)+j(4)
                inv=rcp(s,approx)
                r=r2*lax.rsqrt(jnp.maximum(r2,1e-30))
                i2=inv*inv
                w=jnp.maximum(inv-r*i2,0.0)
                va=jnp.minimum((i(4)-j(5))*dx+(i(5)-j(6))*dy+(i(6)-j(7))*dz,0.0)
                m=s*va*rcp(r2+0.0025*(s*s),approx)
                visc=m*((m-i(7))-e(0))*rcp(i(9)+e(2),approx)
                f=(i(8)+e(1)+visc)*j(3)*((w*w)*(w*i2))
                return f*dx,f*dy,f*dz
            def many(k,total):
                t=first+k*JB
                ts=[tile(t+q) for q in range(JB)]
                return tuple(total[c]+functools.reduce(lambda p,q:p+q,[x[c] for x in ts]) for c in range(3))
            z=jnp.zeros((IB,128),jnp.float32)
            total=lax.fori_loop(0,nfull,many,(z,z,z))
            if JB>1:
                def one(t,tt):
                    x=tile(t)
                    return tuple(p+q for p,q in zip(tt,x))
                total=lax.fori_loop(first+nfull*JB,last,one,total)
            for c in range(3):
                acc[c,a,rows,:]=total[c]
            return 0
        lax.fori_loop(0,(count+IB-1)//IB,iblock,0)
        return 0
    lax.fori_loop(0,CELLS,cell,0)
    for a in range(CELLS):
        for c in range(3):
            sums=jnp.sum(acc[c,a].T,axis=0,keepdims=True)
            out[c,a:a+1,:]=jnp.where(rec[a,3:4,:]>0,(160.0*NORM)*sums,0.0)

def force(rec,snd,rho,meta,tab,buf,IB=32,JB=2,approx=True):
    V=pl.BlockSpec(memory_space=pltpu.VMEM); S=pl.BlockSpec(memory_space=pltpu.SMEM)
    return pl.pallas_call(functools.partial(force_kernel,IB,JB,approx),
        out_shape=jax.ShapeDtypeStruct((3,CELLS,SLOTS),jnp.float32),
        in_specs=[V,V,V,S,S,V],out_specs=V,
        scratch_shapes=[pltpu.VMEM((MAXT,8,128),jnp.float32),pltpu.VMEM((144,8,SLOTS),jnp.float32),pltpu.VMEM((10,SLOTS,128),jnp.float32),pltpu.VMEM((3,CELLS,SLOTS,128),jnp.float32)],
        compiler_params=pltpu.CompilerParams(vmem_limit_bytes=48<<20),
        name="force")(rec,snd,rho,meta,tab,buf)


from jax.sharding import PartitionSpec as P

N_GX=16; N_GY=8
AROUND=((-1,-1),(-1,0),(-1,1),(0,-1),(0,1),(1,-1),(1,0),(1,1))
MESH=pl.DeviceIdType.MESH


def neighbours(u, w):
    return [(lax.rem(u + du + N_GX, N_GX), lax.rem(w + dw + N_GY, N_GY)) for du, dw in AROUND]


def exchange_kernel(pos, vel, mass, smooth, snd, counts, move, lists, rec_out, snd_out, meta_out,
                    rec, outbox, inbox, metas, send1, recv1, send2, recv2):
    u, w = lax.axis_index("gx"), lax.axis_index("gy")
    around = neighbours(u, w)
    barrier = pltpu.get_barrier_semaphore()
    for off in range(1, N_GX):
        pl.semaphore_signal(barrier, inc=1, device_id=(lax.rem(u + off, N_GX), w), device_id_type=MESH)
    for n, (du, dw) in enumerate(AROUND):
        if dw != 0:
            pl.semaphore_signal(barrier, inc=1, device_id=around[n], device_id_type=MESH)

    slot = lax.broadcasted_iota(jnp.int32, (1, 256), 1)
    for c in range(16):
        for f in range(3):
            rec[c, f:f + 1, :] = pos[f, c:c + 1, :]
            rec[c, 5 + f:6 + f, :] = vel[f, c:c + 1, :]
        rec[c, 3:4, :] = jnp.where(slot < counts[c], mass[c:c + 1, :], 0.0)
        rec[c, 4:5, :] = smooth[c:c + 1, :]

    columns = [lax.shift_right_logical(move[c], 7) for c in range(16)]
    row = lax.broadcasted_iota(jnp.int32, (8, 256), 0)

    def post(off, _):
        column = lax.rem(u + off, N_GX)
        first, last = jnp.int32(16), jnp.int32(-1)
        for c in range(16):
            match = columns[c] == column
            first = jnp.minimum(first, jnp.where(match, c, 16))
            last = jnp.where(match, c, last)
        found = last >= 0
        first = jnp.where(found, first, 0)
        last = jnp.where(found, last, 0)
        outbox[off, 0:8, :] = rec[first]
        outbox[off, 8:16, :] = rec[last]
        number = lambda c: jnp.where(found, move[c], -1).astype(jnp.float32)
        amount = lambda c: counts[c].astype(jnp.float32)
        more = jnp.where(row == 0, snd[pl.ds(first, 1), :], snd[pl.ds(last, 1), :])
        more = jnp.where(row == 2, number(first), more)
        more = jnp.where(row == 3, number(last), more)
        more = jnp.where(row == 4, amount(first), more)
        more = jnp.where(row == 5, amount(last), more)
        outbox[off, 16:24, :] = more
        return 0

    lax.fori_loop(0, N_GX, post, 0)
    pl.semaphore_wait(barrier, N_GX - 1 + 6)

    def parcel(off):
        return pltpu.make_async_remote_copy(
            src_ref=outbox.at[off], dst_ref=inbox.at[off], send_sem=send1.at[off], recv_sem=recv1.at[off],
            device_id=(lax.rem(u + off, N_GX), w), device_id_type=MESH)

    def start(off, _):
        parcel(off).start()
        return 0

    lax.fori_loop(1, N_GX, start, 0)
    inbox[0] = outbox[0]

    first_own = ((u * N_GY + w) * 16).astype(jnp.float32)
    sub = lax.broadcasted_iota(jnp.int32, (16, 256), 0).astype(jnp.float32) + first_own
    lane = lax.broadcasted_iota(jnp.int32, (1, 128), 1).astype(jnp.float32) + first_own

    def absorb(off, carry):
        cells, sounds, amounts = carry
        cells = list(cells)
        for k in range(2):
            block = inbox[off, 8 * k:8 * k + 8, :]
            sound = inbox[off, 16 + k:17 + k, :]
            number = inbox[off, 18 + k:19 + k, :]
            amount = inbox[off, 20 + k:21 + k, 0:128]
            sounds = jnp.where(sub == number, sound, sounds)
            amounts = jnp.where(lane == number[:, 0:128], amount, amounts)
            wide = jnp.broadcast_to(number, (8, 256))
            for t in range(16):
                cells[t] = jnp.where(wide == first_own + t, block, cells[t])
        return tuple(cells), sounds, amounts

    def absorb_next(off, carry):
        parcel(off).wait_recv()
        return absorb(off, carry)

    zero = jnp.zeros((8, 256), jnp.float32)
    carry = absorb(0, ((zero,) * 16, jnp.zeros((16, 256), jnp.float32), jnp.zeros((1, 128), jnp.float32)))
    cells, sounds, amounts = lax.fori_loop(1, N_GX, absorb_next, carry)
    for t in range(16):
        rec_out[0, t] = cells[t]
    snd_out[0] = sounds
    amounts = amounts.astype(jnp.int32)
    slot = lax.broadcasted_iota(jnp.int32, (1, 128), 1)
    meta_out[0] = amounts
    for n in range(8):
        metas[n] = jnp.where(slot < 16, amounts, lists[n:n + 1, :])

    copies = []
    for n in range(8):
        for k, (src, dst) in enumerate(((metas.at[n], meta_out.at[n + 1]), (rec_out.at[0], rec_out.at[n + 1]), (snd_out.at[0], snd_out.at[n + 1]))):
            copy = pltpu.make_async_remote_copy(
                src_ref=src, dst_ref=dst, send_sem=send2.at[n, k], recv_sem=recv2.at[n, k],
                device_id=around[n], device_id_type=MESH)
            copy.start()
            copies.append(copy)

    def sent(off, _):
        parcel(off).wait_send()
        return 0

    lax.fori_loop(1, N_GX, sent, 0)
    for copy in copies:
        copy.wait()


VMEM=pl.BlockSpec(memory_space=pltpu.VMEM)
SMEM=pl.BlockSpec(memory_space=pltpu.SMEM)

def exchange(positions, velocities, masses, smoothing, sound2, counts, move_to, lists):
    return pl.pallas_call(
        exchange_kernel,
        out_shape=(jax.ShapeDtypeStruct((9, 16, 8, 256), jnp.float32),
                   jax.ShapeDtypeStruct((9, 16, 256), jnp.float32),
                   jax.ShapeDtypeStruct((9, 1, 128), jnp.int32)),
        in_specs=[VMEM] * 5 + [SMEM] * 2 + [VMEM],
        out_specs=(VMEM,) * 3,
        scratch_shapes=[
            pltpu.VMEM((16, 8, 256), jnp.float32),
            pltpu.VMEM((N_GX, 24, 256), jnp.float32),
            pltpu.VMEM((N_GX, 24, 256), jnp.float32),
            pltpu.VMEM((8, 1, 128), jnp.int32),
            pltpu.SemaphoreType.DMA((N_GX,)),
            pltpu.SemaphoreType.DMA((N_GX,)),
            pltpu.SemaphoreType.DMA((8, 3)),
            pltpu.SemaphoreType.DMA((8, 3)),
        ],
        compiler_params=pltpu.CompilerParams(collective_id=0, has_side_effects=True, vmem_limit_bytes=32 << 20),
        name="exchange",
    )(positions, velocities, masses, smoothing, sound2, counts, move_to, lists)


def share_kernel(own, out, send, recv):
    u, w = lax.axis_index("gx"), lax.axis_index("gy")
    around = neighbours(u, w)
    barrier = pltpu.get_barrier_semaphore()
    for n in range(8):
        pl.semaphore_signal(barrier, inc=1, device_id=around[n], device_id_type=MESH)
    pl.semaphore_wait(barrier, 8)
    copies = []
    for n in range(8):
        copy = pltpu.make_async_remote_copy(
            src_ref=own, dst_ref=out.at[n + 1], send_sem=send.at[n], recv_sem=recv.at[n],
            device_id=around[n], device_id_type=MESH)
        copy.start()
        copies.append(copy)
    out[0] = own[...]
    for copy in copies:
        copy.wait()


def share(own):
    return pl.pallas_call(
        share_kernel,
        out_shape=jax.ShapeDtypeStruct((9, 16, 256), jnp.float32),
        in_specs=[VMEM], out_specs=VMEM,
        scratch_shapes=[pltpu.SemaphoreType.DMA((8,)), pltpu.SemaphoreType.DMA((8,))],
        compiler_params=pltpu.CompilerParams(collective_id=1, has_side_effects=True),
        name="share",
    )(own)


def body(positions, velocities, masses, smoothing, sound2, counts, move_to, proxy_send, pairs):
    lists = jnp.pad(proxy_send.reshape(8, 16), ((0, 0), (16, 96)))
    rec, snd, meta = exchange(positions, velocities, masses, smoothing, sound2, counts, move_to, lists)
    rec = rec.reshape(144, 8, 256)
    meta = meta.reshape(-1)
    rho, safe, tab, buf = density(rec, meta, pairs.reshape(-1))
    rho_all = share(safe)
    accel = force(rec, snd, rho_all, meta, tab, buf)
    return rho, accel


def solution(mesh):
    flat, cells, three = P(("gx", "gy")), P(("gx", "gy"), None), P(None, ("gx", "gy"), None)
    return jax.shard_map(
        body, mesh=mesh,
        in_specs=(three, three, cells, cells, cells, flat, flat, flat, cells),
        out_specs=(cells, three), check_vma=False)
```

```python
import math, functools
import jax, jax.numpy as jnp
from jax import lax
from jax.experimental import pallas as pl
from jax.experimental.pallas import tpu as pltpu

CELLS=16; SLOTS=256; NPAIRS=160; NORM=21.0/(16.0*math.pi)
WHOLE=63<<20
MAXT=2*NPAIRS+3*CELLS+8
PLACE=NPAIRS; FIRST=2*NPAIRS; LAST=FIRST+CELLS

def rcp(x):
    return pl.reciprocal(x, approx=True)

def append(buf, x0, x1, pos, lane):
    tile=lax.shift_right_logical(pos,7); s=lax.bitwise_and(pos,127)
    t0=pltpu.roll(x0,s,1); t1=pltpu.roll(x1,s,1)
    keep=lane>=s
    pltpu.store(buf.at[tile],t0,mask=keep)
    buf[tile+1]=jnp.where(keep,t1,t0)
    buf[tile+2]=jnp.where(keep,0.0,t1)

def plan(meta, pairs, tab, filled, count_of):
    for a in range(CELLS):
        filled[a]=0
    def size(p,_):
        a=pairs[0,p]; b=pairs[1,p]
        n=lax.shift_right_logical(b,4); r=lax.bitwise_and(b,15)
        cell=jnp.where(n==0,r,meta[n,1,jnp.maximum(n-1,0)*16+r])
        count=meta[n,0,cell]
        tab[p]=n*16+cell
        count_of[p]=count
        filled[a]=filled[a]+count
        return 0
    lax.fori_loop(0,NPAIRS,size,0,unroll=8)
    tile=jnp.int32(0)
    for a in range(CELLS):
        end=tile+lax.shift_right_logical(filled[a]+127,7)
        tab[FIRST+a]=tile; tab[LAST+a]=end
        filled[a]=tile*128
        tile=end+2

def pack_main(rec, pairs, tab, filled, count_of, shifts, buf, unroll):
    lane=lax.broadcasted_iota(jnp.int32,(8,128),1)
    row=lax.broadcasted_iota(jnp.int32,(8,128),0)
    for d in range(27):
        dx,dy,dz=d//9-1,d//3%3-1,d%3-1
        shifts[d]=jnp.where(row==0,float(dx),jnp.where(row==1,float(dy),jnp.where(row==2,float(dz),0.0)))
    def put(p,_):
        a=pairs[0,p]
        pos=filled[a]
        filled[a]=pos+count_of[p]
        tab[PLACE+p]=pos
        src=tab[p]; shift=shifts[pairs[2,p]]
        append(buf,rec[src,:,0:128]+shift,rec[src,:,128:256]+shift,pos,lane)
        return 0
    lax.fori_loop(0,NPAIRS,put,0,unroll=unroll)

def spread(icol, f, row):
    for half in range(2):
        part=slice(128*half,128*half+128)
        icol[f,part,:]=jnp.broadcast_to(row[:,part],(128,128)).T

def fetch(pairs_of_refs, sems):
    copies=[pltpu.make_async_copy(src,dst,sems.at[k]) for k,(src,dst) in enumerate(pairs_of_refs)]
    for copy in copies:
        copy.start()
    return copies

def density_kernel(IB,JB,U,rec_in,meta_in,pairs_in,rho,safe,tab,buf_out,rec,meta,pairs,buf,sems,filled,count_of,shifts,icol,acc):
    copies=fetch(((meta_in,meta),(pairs_in,pairs),(rec_in,rec)),sems)
    copies[0].wait(); copies[1].wait()
    plan(meta,pairs,tab,filled,count_of)
    copies[2].wait()
    pack_main(rec,pairs,tab,filled,count_of,shifts,buf,U)
    leave=pltpu.make_async_copy(buf,buf_out,sems.at[3])
    leave.start()
    def cell(a,_):
        for f,rw in enumerate((0,1,2,4)):
            spread(icol,f,rec[a,rw:rw+1,:])
        first=tab[FIRST+a]; last=tab[LAST+a]
        nfull=(last-first)//JB
        count=meta[0,0,a]
        def iblock(g,_):
            rows=pl.ds(pl.multiple_of(g*IB,IB),IB)
            xi,yi,zi,hi=(icol[f,rows,:] for f in range(4))
            def tile(t):
                j=lambda rw: buf[t,rw:rw+1,:]
                dx=xi-j(0); dy=yi-j(1); dz=zi-j(2)
                r2=dx*dx+dy*dy+dz*dz
                s=hi+j(4)
                inv=rcp(s)
                r=r2*lax.rsqrt(jnp.maximum(r2,1e-30))
                w=jnp.maximum(inv-r*(inv*inv),0.0)
                t_=w*s
                return (w*w)*(w*t_)*((1.25-t_)*j(3))
            def many(k,total):
                t=first+k*JB
                return total+functools.reduce(lambda p,q:p+q,[tile(t+i) for i in range(JB)])
            total=lax.fori_loop(0,nfull,many,jnp.zeros((IB,128),jnp.float32))
            if JB>1:
                total=lax.fori_loop(first+nfull*JB,last,lambda t,tt:tt+tile(t),total)
            acc[a,rows,:]=total
            return 0
        lax.fori_loop(0,(count+IB-1)//IB,iblock,0)
        return 0
    lax.fori_loop(0,CELLS,cell,0)
    for a in range(CELLS):
        sums=jnp.sum(acc[a].T,axis=0,keepdims=True)
        there=rec[a,3:4,:]>0
        rho[a:a+1,:]=jnp.where(there,(32.0*NORM)*sums,0.0)
        safe[a:a+1,:]=jnp.where(there,(32.0*NORM)*sums,1.0)
    leave.wait()

def density(rec,meta,pairs,IB=64,JB=2,U=8):
    V=pl.BlockSpec(memory_space=pltpu.VMEM); S=pl.BlockSpec(memory_space=pltpu.SMEM); H=pl.BlockSpec(memory_space=pltpu.HBM)
    return pl.pallas_call(functools.partial(density_kernel,IB,JB,U),
        out_shape=(jax.ShapeDtypeStruct((CELLS,SLOTS),jnp.float32),jax.ShapeDtypeStruct((CELLS,SLOTS),jnp.float32),jax.ShapeDtypeStruct((384,),jnp.int32),jax.ShapeDtypeStruct((MAXT,8,128),jnp.float32)),
        in_specs=[H,H,H],out_specs=(V,V,S,H),
        scratch_shapes=[pltpu.VMEM((144,8,SLOTS),jnp.float32),pltpu.SMEM((9,2,128),jnp.int32),pltpu.SMEM((3,NPAIRS),jnp.int32),pltpu.VMEM((MAXT,8,128),jnp.float32),pltpu.SemaphoreType.DMA((4,)),pltpu.SMEM((CELLS,),jnp.int32),pltpu.SMEM((NPAIRS,),jnp.int32),pltpu.VMEM((27,8,128),jnp.float32),pltpu.VMEM((4,SLOTS,128),jnp.float32),pltpu.VMEM((CELLS,SLOTS,128),jnp.float32)],
        compiler_params=pltpu.CompilerParams(vmem_limit_bytes=WHOLE),
        name="density")(rec,meta,pairs)

def force_kernel(IB,JB,U,rec_in,snd_in,rho_in,meta_in,tab_in,buf_in,out,rec,snd,rho,meta,tab,buf,sems,extra,cells,icol,acc):
    copies=fetch(((snd_in,snd),(rho_in,rho),(tab_in,tab),(meta_in.at[0],meta.at[0]),(rec_in.at[pl.ds(0,CELLS)],rec),(buf_in,buf)),sems)
    for copy in copies[:4]:
        copy.wait()
    for n in range(9):
        for half in range(2):
            c8=slice(8*half,8*half+8)
            c2=snd[n,c8,:]; rr=rho[n,c8,:]
            base=(n*16+8*half)*8
            for f,val in enumerate((0.5*(c2*lax.rsqrt(c2)),c2*rcp(rr),rr)):
                cells[0,pl.ds(base+f,8,stride=8),:]=val[:,0:128]
                cells[1,pl.ds(base+f,8,stride=8),:]=val[:,128:256]
    lane=lax.broadcasted_iota(jnp.int32,(8,128),1)
    block=lambda src: pl.ds(pl.multiple_of(src*8,8),8)
    def put(p,_):
        src=tab[p]
        append(extra,cells[0,block(src),:],cells[1,block(src),:],tab[PLACE+p],lane)
        return 0
    lax.fori_loop(0,NPAIRS,put,0,unroll=U)
    for copy in copies[4:]:
        copy.wait()
    def cell(a,_):
        for f,rw in enumerate((0,1,2,4,5,6,7)):
            spread(icol,f,rec[a,rw:rw+1,:])
        for f in range(3):
            for half in range(2):
                icol[7+f,128*half:128*half+128,:]=jnp.broadcast_to(cells[half,pl.ds(a*8+f,1),:],(128,128)).T
        first=tab[FIRST+a]; last=tab[LAST+a]
        nfull=(last-first)//JB
        count=meta[0,0,a]
        def iblock(g,_):
            rows=pl.ds(pl.multiple_of(g*IB,IB),IB)
            def tile(t):
                i=lambda f: icol[f,rows,:]
                j=lambda rw: buf[t,rw:rw+1,:]
                e=lambda rw: extra[t,rw:rw+1,:]
                dx=i(0)-j(0); dy=i(1)-j(1); dz=i(2)-j(2)
                r2=dx*dx+dy*dy+dz*dz
                s=i(3)+j(4)
                inv=rcp(s)
                r=r2*lax.rsqrt(jnp.maximum(r2,1e-30))
                i2=inv*inv
                w=jnp.maximum(inv-r*i2,0.0)
                va=jnp.minimum((i(4)-j(5))*dx+(i(5)-j(6))*dy+(i(6)-j(7))*dz,0.0)
                m=s*va*rcp(r2+0.0025*(s*s))
                visc=m*((m-i(7))-e(0))*rcp(i(9)+e(2))
                f=(i(8)+e(1)+visc)*j(3)*((w*w)*(w*i2))
                return f*dx,f*dy,f*dz
            def many(k,total):
                t=first+k*JB
                ts=[tile(t+q) for q in range(JB)]
                return tuple(total[c]+functools.reduce(lambda p,q:p+q,[x[c] for x in ts]) for c in range(3))
            z=jnp.zeros((IB,128),jnp.float32)
            total=lax.fori_loop(0,nfull,many,(z,z,z))
            if JB>1:
                def one(t,tt):
                    x=tile(t)
                    return tuple(p+q for p,q in zip(tt,x))
                total=lax.fori_loop(first+nfull*JB,last,one,total)
            for c in range(3):
                acc[c,a,rows,:]=total[c]
            return 0
        lax.fori_loop(0,(count+IB-1)//IB,iblock,0)
        return 0
    lax.fori_loop(0,CELLS,cell,0)
    for a in range(CELLS):
        for c in range(3):
            sums=jnp.sum(acc[c,a].T,axis=0,keepdims=True)
            out[c,a:a+1,:]=jnp.where(rec[a,3:4,:]>0,(160.0*NORM)*sums,0.0)

def force(rec,snd,rho,meta,tab,buf,IB=32,JB=2,U=8):
    V=pl.BlockSpec(memory_space=pltpu.VMEM); S=pl.BlockSpec(memory_space=pltpu.SMEM); H=pl.BlockSpec(memory_space=pltpu.HBM)
    return pl.pallas_call(functools.partial(force_kernel,IB,JB,U),
        out_shape=jax.ShapeDtypeStruct((3,CELLS,SLOTS),jnp.float32),
        in_specs=[H]*6,out_specs=V,
        scratch_shapes=[pltpu.VMEM((CELLS,8,SLOTS),jnp.float32),pltpu.VMEM((9,CELLS,SLOTS),jnp.float32),pltpu.VMEM((9,CELLS,SLOTS),jnp.float32),pltpu.SMEM((1,2,128),jnp.int32),pltpu.SMEM((384,),jnp.int32),pltpu.VMEM((MAXT,8,128),jnp.float32),pltpu.SemaphoreType.DMA((6,)),pltpu.VMEM((MAXT,8,128),jnp.float32),pltpu.VMEM((2,144*8,128),jnp.float32),pltpu.VMEM((10,SLOTS,128),jnp.float32),pltpu.VMEM((3,CELLS,SLOTS,128),jnp.float32)],
        compiler_params=pltpu.CompilerParams(vmem_limit_bytes=WHOLE),
        name="force")(rec,snd,rho,meta,tab,buf)


from jax.sharding import PartitionSpec as P

N_GX=16; N_GY=8
AROUND=((-1,-1),(-1,0),(-1,1),(0,-1),(0,1),(1,-1),(1,0),(1,1))
MESH=pl.DeviceIdType.MESH


def neighbours(u, w):
    return [(lax.rem(u + du + N_GX, N_GX), lax.rem(w + dw + N_GY, N_GY)) for du, dw in AROUND]


def exchange_kernel(*refs):
    given, (rec_out, snd_out, meta_out), scratch = refs[:8], refs[8:11], refs[11:]
    held, (rec, outbox, inbox, metas, moved, sounds_moved, load, send1, recv1, send2, recv2) = scratch[:8], scratch[8:]
    pos, vel, mass, smooth, snd, counts, move, lists = held
    u, w = lax.axis_index("gx"), lax.axis_index("gy")
    loads = [pltpu.make_async_copy(src, dst, load.at[k]) for k, (src, dst) in enumerate(zip(given, held))]
    for copy in loads:
        copy.start()
    around = neighbours(u, w)
    barrier = pltpu.get_barrier_semaphore()
    for off in range(1, N_GX):
        pl.semaphore_signal(barrier, inc=1, device_id=(lax.rem(u + off, N_GX), w), device_id_type=MESH)
    for n, (du, dw) in enumerate(AROUND):
        if dw != 0:
            pl.semaphore_signal(barrier, inc=1, device_id=around[n], device_id_type=MESH)

    for copy in loads:
        copy.wait()
    slot = lax.broadcasted_iota(jnp.int32, (1, 256), 1)
    for c in range(16):
        for f in range(3):
            rec[c, f:f + 1, :] = pos[f, c:c + 1, :]
            rec[c, 5 + f:6 + f, :] = vel[f, c:c + 1, :]
        rec[c, 3:4, :] = jnp.where(slot < counts[c], mass[c:c + 1, :], 0.0)
        rec[c, 4:5, :] = smooth[c:c + 1, :]

    columns = [lax.shift_right_logical(move[c], 7) for c in range(16)]
    row = lax.broadcasted_iota(jnp.int32, (8, 256), 0)

    def post(off, _):
        column = lax.rem(u + off, N_GX)
        first, last = jnp.int32(16), jnp.int32(-1)
        for c in range(16):
            match = columns[c] == column
            first = jnp.minimum(first, jnp.where(match, c, 16))
            last = jnp.where(match, c, last)
        found = last >= 0
        first = jnp.where(found, first, 0)
        last = jnp.where(found, last, 0)
        outbox[off, 0:8, :] = rec[first]
        outbox[off, 8:16, :] = rec[last]
        number = lambda c: jnp.where(found, move[c], -1).astype(jnp.float32)
        amount = lambda c: counts[c].astype(jnp.float32)
        more = jnp.where(row == 0, snd[pl.ds(first, 1), :], snd[pl.ds(last, 1), :])
        more = jnp.where(row == 2, number(first), more)
        more = jnp.where(row == 3, number(last), more)
        more = jnp.where(row == 4, amount(first), more)
        more = jnp.where(row == 5, amount(last), more)
        outbox[off, 16:24, :] = more
        return 0

    lax.fori_loop(0, N_GX, post, 0)
    pl.semaphore_wait(barrier, N_GX - 1 + 6)

    def parcel(off):
        return pltpu.make_async_remote_copy(
            src_ref=outbox.at[off], dst_ref=inbox.at[off], send_sem=send1.at[off], recv_sem=recv1.at[off],
            device_id=(lax.rem(u + off, N_GX), w), device_id_type=MESH)

    def start(off, _):
        parcel(off).start()
        return 0

    lax.fori_loop(1, N_GX, start, 0)
    inbox[0] = outbox[0]

    first_own = ((u * N_GY + w) * 16).astype(jnp.float32)
    sub = lax.broadcasted_iota(jnp.int32, (16, 256), 0).astype(jnp.float32) + first_own
    lane = lax.broadcasted_iota(jnp.int32, (1, 128), 1).astype(jnp.float32) + first_own

    def absorb(off, carry):
        cells, sounds, amounts = carry
        cells = list(cells)
        for k in range(2):
            block = inbox[off, 8 * k:8 * k + 8, :]
            sound = inbox[off, 16 + k:17 + k, :]
            number = inbox[off, 18 + k:19 + k, :]
            amount = inbox[off, 20 + k:21 + k, 0:128]
            sounds = jnp.where(sub == number, sound, sounds)
            amounts = jnp.where(lane == number[:, 0:128], amount, amounts)
            wide = jnp.broadcast_to(number, (8, 256))
            for t in range(16):
                cells[t] = jnp.where(wide == first_own + t, block, cells[t])
        return tuple(cells), sounds, amounts

    def absorb_next(off, carry):
        parcel(off).wait_recv()
        return absorb(off, carry)

    zero = jnp.zeros((8, 256), jnp.float32)
    carry = absorb(0, ((zero,) * 16, jnp.zeros((16, 256), jnp.float32), jnp.zeros((1, 128), jnp.float32)))
    cells, sounds, amounts = lax.fori_loop(1, N_GX, absorb_next, carry)
    for t in range(16):
        moved[t] = cells[t]
    sounds_moved[...] = sounds
    metas[0:1, :] = amounts.astype(jnp.int32)
    metas[1:2, :] = lists[...]

    copies = []
    own = ((metas, meta_out), (moved, rec_out), (sounds_moved, snd_out))
    for n in range(8):
        for k, (src, dst) in enumerate(own):
            copy = pltpu.make_async_remote_copy(
                src_ref=src, dst_ref=dst.at[n + 1], send_sem=send2.at[n, k], recv_sem=recv2.at[n, k],
                device_id=around[n], device_id_type=MESH)
            copy.start()
            copies.append(copy)
    for k, (src, dst) in enumerate(own):
        copy = pltpu.make_async_copy(src, dst.at[0], load.at[k])
        copy.start()
        copies.append(copy)

    def sent(off, _):
        parcel(off).wait_send()
        return 0

    lax.fori_loop(1, N_GX, sent, 0)
    for copy in copies:
        copy.wait()


VMEM=pl.BlockSpec(memory_space=pltpu.VMEM)
HBM=pl.BlockSpec(memory_space=pltpu.HBM)

def exchange(positions, velocities, masses, smoothing, sound2, counts, move_to, lists):
    return pl.pallas_call(
        exchange_kernel,
        out_shape=(jax.ShapeDtypeStruct((9, 16, 8, 256), jnp.float32),
                   jax.ShapeDtypeStruct((9, 16, 256), jnp.float32),
                   jax.ShapeDtypeStruct((9, 2, 128), jnp.int32)),
        in_specs=[HBM] * 8,
        out_specs=(HBM,) * 3,
        scratch_shapes=[
            pltpu.VMEM((3, 16, 256), jnp.float32),
            pltpu.VMEM((3, 16, 256), jnp.float32),
            pltpu.VMEM((16, 256), jnp.float32),
            pltpu.VMEM((16, 256), jnp.float32),
            pltpu.VMEM((16, 256), jnp.float32),
            pltpu.SMEM((16,), jnp.int32),
            pltpu.SMEM((16,), jnp.int32),
            pltpu.VMEM((1, 128), jnp.int32),
            pltpu.VMEM((16, 8, 256), jnp.float32),
            pltpu.VMEM((N_GX, 24, 256), jnp.float32),
            pltpu.VMEM((N_GX, 24, 256), jnp.float32),
            pltpu.VMEM((2, 128), jnp.int32),
            pltpu.VMEM((16, 8, 256), jnp.float32),
            pltpu.VMEM((16, 256), jnp.float32),
            pltpu.SemaphoreType.DMA((8,)),
            pltpu.SemaphoreType.DMA((N_GX,)),
            pltpu.SemaphoreType.DMA((N_GX,)),
            pltpu.SemaphoreType.DMA((8, 3)),
            pltpu.SemaphoreType.DMA((8, 3)),
        ],
        compiler_params=pltpu.CompilerParams(collective_id=0, has_side_effects=True, vmem_limit_bytes=WHOLE),
        name="exchange",
    )(positions, velocities, masses, smoothing, sound2, counts, move_to, lists)


def share_kernel(own, out, load, send, recv):
    u, w = lax.axis_index("gx"), lax.axis_index("gy")
    around = neighbours(u, w)
    barrier = pltpu.get_barrier_semaphore()
    for n in range(8):
        pl.semaphore_signal(barrier, inc=1, device_id=around[n], device_id_type=MESH)
    copies = [pltpu.make_async_copy(own, out.at[0], load)]
    copies[0].start()
    pl.semaphore_wait(barrier, 8)
    for n in range(8):
        copy = pltpu.make_async_remote_copy(
            src_ref=own, dst_ref=out.at[n + 1], send_sem=send.at[n], recv_sem=recv.at[n],
            device_id=around[n], device_id_type=MESH)
        copy.start()
        copies.append(copy)
    for copy in copies:
        copy.wait()


def share(own):
    return pl.pallas_call(
        share_kernel,
        out_shape=jax.ShapeDtypeStruct((9, 16, 256), jnp.float32),
        in_specs=[HBM], out_specs=HBM,
        scratch_shapes=[pltpu.SemaphoreType.DMA, pltpu.SemaphoreType.DMA((8,)), pltpu.SemaphoreType.DMA((8,))],
        compiler_params=pltpu.CompilerParams(collective_id=1, has_side_effects=True, vmem_limit_bytes=WHOLE),
        name="share",
    )(own)


def body(positions, velocities, masses, smoothing, sound2, counts, move_to, proxy_send, pairs):
    rec, snd, meta = exchange(positions, velocities, masses, smoothing, sound2, counts, move_to, proxy_send.reshape(1, 128))
    rec = rec.reshape(144, 8, 256)
    rho, safe, tab, buf = density(rec, meta, pairs.T)
    rho_all = share(safe)
    accel = force(rec, snd, rho_all, meta, tab, buf)
    return rho, accel


def solution(mesh):
    flat, cells, three = P(("gx", "gy")), P(("gx", "gy"), None), P(None, ("gx", "gy"), None)
    return jax.shard_map(
        body, mesh=mesh,
        in_specs=(three, three, cells, cells, cells, flat, flat, flat, cells),
        out_specs=(cells, three), check_vma=False)
```

```python
import math, functools
import jax, jax.numpy as jnp
from jax import lax
from jax.experimental import pallas as pl
from jax.experimental.pallas import tpu as pltpu

CELLS=16; SLOTS=256; NPAIRS=160; NORM=21.0/(16.0*math.pi)
WHOLE=63<<20
MAXT=2*NPAIRS+3*CELLS+8
PLACE=NPAIRS; FIRST=2*NPAIRS; LAST=FIRST+CELLS

def rcp(x):
    return pl.reciprocal(x, approx=True)

def append(buf, x0, x1, pos, lane):
    tile=lax.shift_right_logical(pos,7); s=lax.bitwise_and(pos,127)
    t0=pltpu.roll(x0,s,1); t1=pltpu.roll(x1,s,1)
    keep=lane>=s
    pltpu.store(buf.at[tile],t0,mask=keep)
    buf[tile+1]=jnp.where(keep,t1,t0)
    buf[tile+2]=jnp.where(keep,0.0,t1)

def plan(meta, pairs, tab, filled, count_of):
    for a in range(CELLS):
        filled[a]=0
    def size(p,_):
        a=pairs[0,p]; b=pairs[1,p]
        n=lax.shift_right_logical(b,4); r=lax.bitwise_and(b,15)
        cell=jnp.where(n==0,r,meta[n,1,jnp.maximum(n-1,0)*16+r])
        count=meta[n,0,cell]
        tab[p]=n*16+cell
        count_of[p]=count
        filled[a]=filled[a]+count
        return 0
    lax.fori_loop(0,NPAIRS,size,0,unroll=8)
    tile=jnp.int32(0)
    for a in range(CELLS):
        end=tile+lax.shift_right_logical(filled[a]+127,7)
        tab[FIRST+a]=tile; tab[LAST+a]=end
        filled[a]=tile*128
        tile=end+2

def pack_main(rec, pairs, tab, filled, count_of, shifts, buf, unroll):
    lane=lax.broadcasted_iota(jnp.int32,(8,128),1)
    row=lax.broadcasted_iota(jnp.int32,(8,128),0)
    for d in range(27):
        dx,dy,dz=d//9-1,d//3%3-1,d%3-1
        shifts[d]=jnp.where(row==0,float(dx),jnp.where(row==1,float(dy),jnp.where(row==2,float(dz),0.0)))
    def put(p,_):
        a=pairs[0,p]
        pos=filled[a]
        filled[a]=pos+count_of[p]
        tab[PLACE+p]=pos
        src=tab[p]; shift=shifts[pairs[2,p]]
        append(buf,rec[src,:,0:128]+shift,rec[src,:,128:256]+shift,pos,lane)
        return 0
    lax.fori_loop(0,NPAIRS,put,0,unroll=unroll)

def split3(v):
    high=v.astype(jnp.bfloat16)
    rest=v-high.astype(jnp.float32)
    middle=rest.astype(jnp.bfloat16)
    return high,middle,(rest-middle.astype(jnp.float32)).astype(jnp.bfloat16)

def pick(height, left, right):
    k=lax.rem(lax.broadcasted_iota(jnp.int32,(3*height,256),0),height)
    lane=lax.broadcasted_iota(jnp.int32,(3*height,256),1)
    return (k==jnp.where(lane<128,left,right)).astype(jnp.float32).astype(jnp.bfloat16)

def columns(icol, block, rows, by_matrix):
    height=block.shape[0]
    parts=jnp.concatenate(split3(block),0)
    for f in range(0,by_matrix,2):
        both=lax.dot_general(parts,pick(height,rows[f],rows[f+1]),(((0,),(0,)),((),())),preferred_element_type=jnp.float32)
        icol[f]=both[:,0:128]
        icol[f+1]=both[:,128:256]
    for f in range(by_matrix,len(rows)):
        for half in range(2):
            lanes=slice(128*half,128*half+128)
            icol[f,lanes,:]=jnp.broadcast_to(block[rows[f]:rows[f]+1,lanes],(128,128)).T

def fetch(pairs_of_refs, sems):
    copies=[pltpu.make_async_copy(src,dst,sems.at[k]) for k,(src,dst) in enumerate(pairs_of_refs)]
    for copy in copies:
        copy.start()
    return copies

def density_kernel(MD,J64,J32,J16,U,rec_in,meta_in,pairs_in,rho,safe,tab,buf_out,rec,meta,pairs,buf,sems,filled,count_of,shifts,icol,acc):
    copies=fetch(((meta_in,meta),(pairs_in,pairs),(rec_in,rec)),sems)
    copies[0].wait(); copies[1].wait()
    plan(meta,pairs,tab,filled,count_of)
    copies[2].wait()
    pack_main(rec,pairs,tab,filled,count_of,shifts,buf,U)
    leave=pltpu.make_async_copy(buf,buf_out,sems.at[3])
    leave.start()
    def cell(a,_):
        columns(icol,rec[a],(0,1,2,4),MD)
        first=tab[FIRST+a]; last=tab[LAST+a]
        count=meta[0,0,a]
        def iblock(IB,JB,start,_):
            rows=pl.ds(pl.multiple_of(start,16),IB)
            nfull=(last-first)//JB
            xi,yi,zi,hi=(icol[f,rows,:] for f in range(4))
            def tile(t):
                j=lambda rw: buf[t,rw:rw+1,:]
                dx=xi-j(0); dy=yi-j(1); dz=zi-j(2)
                r2=dx*dx+dy*dy+dz*dz
                s=hi+j(4)
                u=rcp(s*lax.rsqrt(r2))
                t_=jnp.maximum(1.0-u,0.0)
                w=t_*rcp(s)
                return (w*w)*(w*t_)*((1.25-t_)*j(3))
            def many(k,total):
                t=first+k*JB
                return total+functools.reduce(lambda p,q:p+q,[tile(t+i) for i in range(JB)])
            total=lax.fori_loop(0,nfull,many,jnp.zeros((IB,128),jnp.float32))
            if JB>1:
                total=lax.fori_loop(first+nfull*JB,last,lambda t,tt:tt+tile(t),total)
            acc[a,rows,:]=total
            return 0
        groups=lax.shift_right_logical(count+15,4)
        rest=lax.bitwise_and(groups,3)
        big=lax.shift_right_logical(groups+1,2)
        lax.fori_loop(0,big,lambda g,c:iblock(64,J64,g*64,c),0)
        lax.fori_loop(0,jnp.where(rest==2,1,0),lambda g,c:iblock(32,J32,big*64,c),0)
        lax.fori_loop(0,jnp.where(rest==1,1,0),lambda g,c:iblock(16,J16,big*64,c),0)
        return 0
    lax.fori_loop(0,CELLS,cell,0)
    for a in range(CELLS):
        sums=jnp.sum(acc[a].T,axis=0,keepdims=True)
        there=rec[a,3:4,:]>0
        rho[a:a+1,:]=jnp.where(there,(32.0*NORM)*sums,0.0)
        safe[a:a+1,:]=jnp.where(there,(32.0*NORM)*sums,1.0)
    leave.wait()

def density(rec,meta,pairs,J64=2,J32=4,J16=4,U=8,M_=None):
    V=pl.BlockSpec(memory_space=pltpu.VMEM); S=pl.BlockSpec(memory_space=pltpu.SMEM); H=pl.BlockSpec(memory_space=pltpu.HBM)
    return pl.pallas_call(functools.partial(density_kernel,0 if M_ is None else M_,J64,J32,J16,U),
        out_shape=(jax.ShapeDtypeStruct((CELLS,SLOTS),jnp.float32),jax.ShapeDtypeStruct((CELLS,SLOTS),jnp.float32),jax.ShapeDtypeStruct((384,),jnp.int32),jax.ShapeDtypeStruct((MAXT,8,128),jnp.float32)),
        in_specs=[H,H,H],out_specs=(V,V,S,H),
        scratch_shapes=[pltpu.VMEM((144,8,SLOTS),jnp.float32),pltpu.SMEM((9,2,128),jnp.int32),pltpu.SMEM((3,NPAIRS),jnp.int32),pltpu.VMEM((MAXT,8,128),jnp.float32),pltpu.SemaphoreType.DMA((4,)),pltpu.SMEM((CELLS,),jnp.int32),pltpu.SMEM((NPAIRS,),jnp.int32),pltpu.VMEM((27,8,128),jnp.float32),pltpu.VMEM((4,SLOTS,128),jnp.float32),pltpu.VMEM((CELLS,SLOTS,128),jnp.float32)],
        compiler_params=pltpu.CompilerParams(vmem_limit_bytes=WHOLE),
        name="density")(rec,meta,pairs)

def force_kernel(MF,J32,J16,U,rec_in,snd_in,rho_in,meta_in,tab_in,buf_in,out,rec,snd,rho,meta,tab,buf,sems,extra,cells,icol,acc):
    copies=fetch(((snd_in,snd),(rho_in,rho),(tab_in,tab),(meta_in.at[0],meta.at[0]),(rec_in.at[pl.ds(0,CELLS)],rec),(buf_in,buf)),sems)
    for copy in copies[:4]:
        copy.wait()
    for n in range(9):
        for half in range(2):
            c8=slice(8*half,8*half+8)
            c2=snd[n,c8,:]; rr=rho[n,c8,:]
            base=(n*16+8*half)*8
            for f,val in enumerate((0.5*(c2*lax.rsqrt(c2)),c2*rcp(rr),rr)):
                cells[0,pl.ds(base+f,8,stride=8),:]=val[:,0:128]
                cells[1,pl.ds(base+f,8,stride=8),:]=val[:,128:256]
    lane=lax.broadcasted_iota(jnp.int32,(8,128),1)
    block=lambda src: pl.ds(pl.multiple_of(src*8,8),8)
    def put(p,_):
        src=tab[p]
        append(extra,cells[0,block(src),:],cells[1,block(src),:],tab[PLACE+p],lane)
        return 0
    lax.fori_loop(0,NPAIRS,put,0,unroll=U)
    for copy in copies[4:]:
        copy.wait()
    def cell(a,_):
        own=pl.ds(pl.multiple_of(a*8,8),8)
        more=jnp.concatenate([cells[0,own,:],cells[1,own,:]],1)
        more=jnp.where(lax.broadcasted_iota(jnp.int32,(8,SLOTS),0)<3,more,0.0)
        columns(icol,jnp.concatenate([rec[a],more],0),(0,1,2,4,5,6,7,8,9,10),MF)
        first=tab[FIRST+a]; last=tab[LAST+a]
        count=meta[0,0,a]
        def iblock(IB,JB,start,_):
            rows=pl.ds(pl.multiple_of(start,16),IB)
            nfull=(last-first)//JB
            def tile(t):
                i=lambda f: icol[f,rows,:]
                j=lambda rw: buf[t,rw:rw+1,:]
                e=lambda rw: extra[t,rw:rw+1,:]
                dx=i(0)-j(0); dy=i(1)-j(1); dz=i(2)-j(2)
                r2=dx*dx+dy*dy+dz*dz
                s=i(3)+j(4)
                inv=rcp(s)
                u=rcp(s*lax.rsqrt(r2))
                w=jnp.maximum(1.0-u,0.0)*inv
                va=jnp.minimum((i(4)-j(5))*dx+(i(5)-j(6))*dy+(i(6)-j(7))*dz,0.0)
                m=va*inv*rcp(u*u+0.0025)
                visc=m*((m-i(7))-e(0))*rcp(i(9)+e(2))
                f=(i(8)+e(1)+visc)*j(3)*((w*w)*(w*(inv*inv)))
                return f*dx,f*dy,f*dz
            def many(k,total):
                t=first+k*JB
                ts=[tile(t+q) for q in range(JB)]
                return tuple(total[c]+functools.reduce(lambda p,q:p+q,[x[c] for x in ts]) for c in range(3))
            z=jnp.zeros((IB,128),jnp.float32)
            total=lax.fori_loop(0,nfull,many,(z,z,z))
            if JB>1:
                def one(t,tt):
                    x=tile(t)
                    return tuple(p+q for p,q in zip(tt,x))
                total=lax.fori_loop(first+nfull*JB,last,one,total)
            for c in range(3):
                acc[c,a,rows,:]=total[c]
            return 0
        groups=lax.shift_right_logical(count+15,4)
        big=lax.shift_right_logical(groups,1)
        lax.fori_loop(0,big,lambda g,c:iblock(32,J32,g*32,c),0)
        lax.fori_loop(0,lax.bitwise_and(groups,1),lambda g,c:iblock(16,J16,big*32,c),0)
        return 0
    lax.fori_loop(0,CELLS,cell,0)
    for a in range(CELLS):
        for c in range(3):
            sums=jnp.sum(acc[c,a].T,axis=0,keepdims=True)
            out[c,a:a+1,:]=jnp.where(rec[a,3:4,:]>0,(160.0*NORM)*sums,0.0)

def force(rec,snd,rho,meta,tab,buf,J32=4,J16=4,U=8,M_=None):
    V=pl.BlockSpec(memory_space=pltpu.VMEM); S=pl.BlockSpec(memory_space=pltpu.SMEM); H=pl.BlockSpec(memory_space=pltpu.HBM)
    return pl.pallas_call(functools.partial(force_kernel,6 if M_ is None else M_,J32,J16,U),
        out_shape=jax.ShapeDtypeStruct((3,CELLS,SLOTS),jnp.float32),
        in_specs=[H]*6,out_specs=V,
        scratch_shapes=[pltpu.VMEM((CELLS,8,SLOTS),jnp.float32),pltpu.VMEM((9,CELLS,SLOTS),jnp.float32),pltpu.VMEM((9,CELLS,SLOTS),jnp.float32),pltpu.SMEM((1,2,128),jnp.int32),pltpu.SMEM((384,),jnp.int32),pltpu.VMEM((MAXT,8,128),jnp.float32),pltpu.SemaphoreType.DMA((6,)),pltpu.VMEM((MAXT,8,128),jnp.float32),pltpu.VMEM((2,144*8,128),jnp.float32),pltpu.VMEM((10,SLOTS,128),jnp.float32),pltpu.VMEM((3,CELLS,SLOTS,128),jnp.float32)],
        compiler_params=pltpu.CompilerParams(vmem_limit_bytes=WHOLE),
        name="force")(rec,snd,rho,meta,tab,buf)


from jax.sharding import PartitionSpec as P

N_GX=16; N_GY=8
AROUND=((-1,-1),(-1,0),(-1,1),(0,-1),(0,1),(1,-1),(1,0),(1,1))
MESH=pl.DeviceIdType.MESH
ITEMS=(0, 1, 2, 3)


def neighbours(u, w):
    return [(lax.rem(u + du + N_GX, N_GX), lax.rem(w + dw + N_GY, N_GY)) for du, dw in AROUND]


def exchange_kernel(*refs):
    given, (rec_out, snd_out, meta_out), scratch = refs[:8], refs[8:11], refs[11:]
    held, (rec, outbox, inbox, metas, moved, sounds_moved, load, send1, recv1, send2, recv2) = scratch[:8], scratch[8:]
    pos, vel, mass, smooth, snd, counts, move, lists = held
    u, w = lax.axis_index("gx"), lax.axis_index("gy")
    loads = [pltpu.make_async_copy(src, dst, load.at[k]) for k, (src, dst) in enumerate(zip(given, held))]
    for copy in loads:
        copy.start()
    around = neighbours(u, w)
    barrier = pltpu.get_barrier_semaphore()
    for off in range(1, N_GX):
        pl.semaphore_signal(barrier, inc=1, device_id=(lax.rem(u + off, N_GX), w), device_id_type=MESH)
    for n in (3, 4):
        pl.semaphore_signal(barrier, inc=1, device_id=around[n], device_id_type=MESH)

    for copy in loads:
        copy.wait()
    slot = lax.broadcasted_iota(jnp.int32, (1, 256), 1)
    for c in range(16):
        for f in range(3):
            rec[c, f:f + 1, :] = pos[f, c:c + 1, :]
            rec[c, 5 + f:6 + f, :] = vel[f, c:c + 1, :]
        rec[c, 3:4, :] = jnp.where(slot < counts[c], mass[c:c + 1, :], 0.0)
        rec[c, 4:5, :] = smooth[c:c + 1, :]

    columns = [lax.shift_right_logical(move[c], 7) for c in range(16)]
    row = lax.broadcasted_iota(jnp.int32, (8, 256), 0)

    def post(off, _):
        column = lax.rem(u + off, N_GX)
        first, last = jnp.int32(16), jnp.int32(-1)
        for c in range(16):
            match = columns[c] == column
            first = jnp.minimum(first, jnp.where(match, c, 16))
            last = jnp.where(match, c, last)
        found = last >= 0
        first = jnp.where(found, first, 0)
        last = jnp.where(found, last, 0)
        outbox[off, 0:8, :] = rec[first]
        outbox[off, 8:16, :] = rec[last]
        number = lambda c: jnp.where(found, move[c], -1).astype(jnp.float32)
        amount = lambda c: counts[c].astype(jnp.float32)
        more = jnp.where(row == 0, snd[pl.ds(first, 1), :], snd[pl.ds(last, 1), :])
        more = jnp.where(row == 2, number(first), more)
        more = jnp.where(row == 3, number(last), more)
        more = jnp.where(row == 4, amount(first), more)
        more = jnp.where(row == 5, amount(last), more)
        outbox[off, 16:24, :] = more
        return 0

    lax.fori_loop(0, N_GX, post, 0)
    pl.semaphore_wait(barrier, N_GX - 1 + 2)

    def parcel(off):
        return pltpu.make_async_remote_copy(
            src_ref=outbox.at[off], dst_ref=inbox.at[off], send_sem=send1.at[off], recv_sem=recv1.at[off],
            device_id=(lax.rem(u + off, N_GX), w), device_id_type=MESH)

    def start(off, _):
        parcel(off).start()
        return 0

    lax.fori_loop(1, N_GX, start, 0)
    inbox[0] = outbox[0]

    first_own = ((u * N_GY + w) * 16).astype(jnp.float32)
    sub = lax.broadcasted_iota(jnp.int32, (16, 256), 0).astype(jnp.float32) + first_own
    lane = lax.broadcasted_iota(jnp.int32, (1, 128), 1).astype(jnp.float32) + first_own

    def absorb(off, carry):
        cells, sounds, amounts = carry
        cells = list(cells)
        for k in range(2):
            block = inbox[off, 8 * k:8 * k + 8, :]
            sound = inbox[off, 16 + k:17 + k, :]
            number = inbox[off, 18 + k:19 + k, :]
            amount = inbox[off, 20 + k:21 + k, 0:128]
            sounds = jnp.where(sub == number, sound, sounds)
            amounts = jnp.where(lane == number[:, 0:128], amount, amounts)
            wide = jnp.broadcast_to(number, (8, 256))
            for t in range(16):
                cells[t] = jnp.where(wide == first_own + t, block, cells[t])
        return tuple(cells), sounds, amounts

    def absorb_next(off, carry):
        parcel(off).wait_recv()
        return absorb(off, carry)

    zero = jnp.zeros((8, 256), jnp.float32)
    carry = absorb(0, ((zero,) * 16, jnp.zeros((16, 256), jnp.float32), jnp.zeros((1, 128), jnp.float32)))
    cells, sounds, amounts = lax.fori_loop(1, N_GX, absorb_next, carry)
    for t in range(16):
        moved[t] = cells[t]
    sounds_moved[...] = sounds
    metas[0:1, :] = amounts.astype(jnp.int32)
    metas[1:2, :] = lists[...]

    halves = (pl.ds(0, 8), pl.ds(8, 8))
    own = (metas, moved.at[halves[0]], moved.at[halves[1]], sounds_moved)
    at = lambda n: (meta_out.at[n], rec_out.at[n, halves[0]], rec_out.at[n, halves[1]], snd_out.at[n])
    remote = lambda src, n, k, device: pltpu.make_async_remote_copy(
        src_ref=src, dst_ref=at(n + 1)[k], send_sem=send2.at[n, k], recv_sem=recv2.at[n, k],
        device_id=device, device_id_type=MESH)
    copies, arriving = [], {}
    for k in ITEMS:
        for n in (1, 6):
            copy = remote(own[k], n, k, around[n])
            copy.start()
            arriving[n, k] = copy
    for k in ITEMS:
        for n in (3, 4):
            copy = remote(own[k], n, k, around[n])
            copy.start()
            copies.append(copy)
    for k in range(4):
        copy = pltpu.make_async_copy(own[k], at(0)[k], load.at[k])
        copy.start()
        copies.append(copy)
    for k in ITEMS:
        for n in (1, 6):
            arriving[n, k].wait_recv()
            for to, step in ((n - 1, 3), (n + 1, 4)):
                copy = remote(at(n + 1)[k], to, k, around[step])
                copy.start()
                copies.append(copy)
    for copy in arriving.values():
        copy.wait_send()

    def sent(off, _):
        parcel(off).wait_send()
        return 0

    lax.fori_loop(1, N_GX, sent, 0)
    for copy in copies:
        copy.wait()


VMEM=pl.BlockSpec(memory_space=pltpu.VMEM)
HBM=pl.BlockSpec(memory_space=pltpu.HBM)

def exchange(positions, velocities, masses, smoothing, sound2, counts, move_to, lists):
    return pl.pallas_call(
        exchange_kernel,
        out_shape=(jax.ShapeDtypeStruct((9, 16, 8, 256), jnp.float32),
                   jax.ShapeDtypeStruct((9, 16, 256), jnp.float32),
                   jax.ShapeDtypeStruct((9, 2, 128), jnp.int32)),
        in_specs=[HBM] * 8,
        out_specs=(HBM,) * 3,
        scratch_shapes=[
            pltpu.VMEM((3, 16, 256), jnp.float32),
            pltpu.VMEM((3, 16, 256), jnp.float32),
            pltpu.VMEM((16, 256), jnp.float32),
            pltpu.VMEM((16, 256), jnp.float32),
            pltpu.VMEM((16, 256), jnp.float32),
            pltpu.SMEM((16,), jnp.int32),
            pltpu.SMEM((16,), jnp.int32),
            pltpu.VMEM((1, 128), jnp.int32),
            pltpu.VMEM((16, 8, 256), jnp.float32),
            pltpu.VMEM((N_GX, 24, 256), jnp.float32),
            pltpu.VMEM((N_GX, 24, 256), jnp.float32),
            pltpu.VMEM((2, 128), jnp.int32),
            pltpu.VMEM((16, 8, 256), jnp.float32),
            pltpu.VMEM((16, 256), jnp.float32),
            pltpu.SemaphoreType.DMA((8,)),
            pltpu.SemaphoreType.DMA((N_GX,)),
            pltpu.SemaphoreType.DMA((N_GX,)),
            pltpu.SemaphoreType.DMA((8, 4)),
            pltpu.SemaphoreType.DMA((8, 4)),
        ],
        compiler_params=pltpu.CompilerParams(collective_id=0, has_side_effects=True, vmem_limit_bytes=WHOLE),
        name="exchange",
    )(positions, velocities, masses, smoothing, sound2, counts, move_to, lists)


def share_kernel(own, out, load, send, recv):
    u, w = lax.axis_index("gx"), lax.axis_index("gy")
    around = neighbours(u, w)
    barrier = pltpu.get_barrier_semaphore()
    for n in range(8):
        pl.semaphore_signal(barrier, inc=1, device_id=around[n], device_id_type=MESH)
    copies = [pltpu.make_async_copy(own, out.at[0], load)]
    copies[0].start()
    pl.semaphore_wait(barrier, 8)
    for n in range(8):
        copy = pltpu.make_async_remote_copy(
            src_ref=own, dst_ref=out.at[n + 1], send_sem=send.at[n], recv_sem=recv.at[n],
            device_id=around[n], device_id_type=MESH)
        copy.start()
        copies.append(copy)
    for copy in copies:
        copy.wait()


def share(own):
    return pl.pallas_call(
        share_kernel,
        out_shape=jax.ShapeDtypeStruct((9, 16, 256), jnp.float32),
        in_specs=[HBM], out_specs=HBM,
        scratch_shapes=[pltpu.SemaphoreType.DMA, pltpu.SemaphoreType.DMA((8,)), pltpu.SemaphoreType.DMA((8,))],
        compiler_params=pltpu.CompilerParams(collective_id=1, has_side_effects=True, vmem_limit_bytes=WHOLE),
        name="share",
    )(own)


def body(positions, velocities, masses, smoothing, sound2, counts, move_to, proxy_send, pairs):
    rec, snd, meta = exchange(positions, velocities, masses, smoothing, sound2, counts, move_to, proxy_send.reshape(1, 128))
    rec = rec.reshape(144, 8, 256)
    rho, safe, tab, buf = density(rec, meta, pairs.T)
    rho_all = share(safe)
    accel = force(rec, snd, rho_all, meta, tab, buf)
    return rho, accel


def solution(mesh):
    flat, cells, three = P(("gx", "gy")), P(("gx", "gy"), None), P(None, ("gx", "gy"), None)
    return jax.shard_map(
        body, mesh=mesh,
        in_specs=(three, three, cells, cells, cells, flat, flat, flat, cells),
        out_specs=(cells, three), check_vma=False)
```

```python
import math, functools
import jax, jax.numpy as jnp
from jax import lax
from jax.experimental import pallas as pl
from jax.experimental.pallas import tpu as pltpu

CELLS=16; SLOTS=256; NPAIRS=160; NORM=21.0/(16.0*math.pi)
WHOLE=63<<20
MAXT=2*NPAIRS+3*CELLS+8
PLACE=NPAIRS; FIRST=2*NPAIRS; LAST=FIRST+CELLS

def rcp(x):
    return pl.reciprocal(x, approx=True)

def append(buf, x0, x1, pos, lane):
    tile=lax.shift_right_logical(pos,7); s=lax.bitwise_and(pos,127)
    t0=pltpu.roll(x0,s,1); t1=pltpu.roll(x1,s,1)
    keep=lane>=s
    pltpu.store(buf.at[tile],t0,mask=keep)
    buf[tile+1]=jnp.where(keep,t1,t0)
    buf[tile+2]=jnp.where(keep,0.0,t1)

def plan(meta, pairs, tab, filled, count_of, place_of):
    for a in range(CELLS):
        filled[a]=0
    def size(p,_):
        a=pairs[0,p]; b=pairs[1,p]
        n=lax.shift_right_logical(b,4); r=lax.bitwise_and(b,15)
        cell=jnp.where(n==0,r,meta[n,1,jnp.maximum(n-1,0)*16+r])
        count=meta[n,0,cell]
        tab[p]=n*16+cell
        place_of[p]=n*16+meta[n,2,cell]
        count_of[p]=count
        filled[a]=filled[a]+count
        return 0
    lax.fori_loop(0,NPAIRS,size,0,unroll=8)
    tile=jnp.int32(0)
    for a in range(CELLS):
        end=tile+lax.shift_right_logical(filled[a]+127,7)
        tab[FIRST+a]=tile; tab[LAST+a]=end
        filled[a]=tile*128
        tile=end+2

def pack_main(rec, pairs, tab, filled, count_of, place_of, shifts, buf, unroll):
    lane=lax.broadcasted_iota(jnp.int32,(8,128),1)
    row=lax.broadcasted_iota(jnp.int32,(8,128),0)
    for d in range(27):
        dx,dy,dz=d//9-1,d//3%3-1,d%3-1
        shifts[d]=jnp.where(row==0,float(dx),jnp.where(row==1,float(dy),jnp.where(row==2,float(dz),0.0)))
    def put(p,_):
        a=pairs[0,p]
        pos=filled[a]
        filled[a]=pos+count_of[p]
        tab[PLACE+p]=pos
        src=place_of[p]; shift=shifts[pairs[2,p]]
        append(buf,rec[src,:,0:128]+shift,rec[src,:,128:256]+shift,pos,lane)
        return 0
    lax.fori_loop(0,NPAIRS,put,0,unroll=unroll)

def columns(icol, block, rows):
    for f,row in enumerate(rows):
        for half in range(2):
            lanes=slice(128*half,128*half+128)
            icol[f,lanes,:]=jnp.broadcast_to(block[row:row+1,lanes],(128,128)).T

def extra_fields(c2, rho):
    return 0.5*(c2*lax.rsqrt(c2)),c2*rcp(rho),rho

def fetch(pairs_of_refs, sems):
    copies=[pltpu.make_async_copy(src,dst,sems.at[k]) for k,(src,dst) in enumerate(pairs_of_refs)]
    for copy in copies:
        copy.start()
    return copies

def density_kernel(J64,J32,J16,U,rec_in,meta_in,pairs_in,cols_in,rho,safe,tab,buf_out,rec,meta,pairs,buf,sems,filled,count_of,place_of,shifts,cols,col_sems,acc):
    copies=fetch(((meta_in,meta),(pairs_in,pairs),(rec_in,rec)),sems)
    copies[0].wait(); copies[1].wait()
    def column_copy(a):
        return pltpu.make_async_copy(cols_in.at[meta[0,2,a],pl.ds(0,4)],cols.at[a],col_sems.at[a])
    def ask(a,_):
        column_copy(a).start()
        return 0
    lax.fori_loop(0,CELLS,ask,0)
    plan(meta,pairs,tab,filled,count_of,place_of)
    copies[2].wait()
    pack_main(rec,pairs,tab,filled,count_of,place_of,shifts,buf,U)
    leave=pltpu.make_async_copy(buf,buf_out,sems.at[3])
    leave.start()
    def cell(a,_):
        column_copy(a).wait()
        icol=cols.at[a]
        first=tab[FIRST+a]; last=tab[LAST+a]
        count=meta[0,0,a]
        def iblock(IB,JB,start,_):
            rows=pl.ds(pl.multiple_of(start,16),IB)
            nfull=(last-first)//JB
            xi,yi,zi,hi=(icol[f,rows,:] for f in range(4))
            def tile(t):
                j=lambda rw: buf[t,rw:rw+1,:]
                dx=xi-j(0); dy=yi-j(1); dz=zi-j(2)
                r2=dx*dx+dy*dy+dz*dz
                s=hi+j(4)
                u=rcp(s*lax.rsqrt(r2))
                t_=jnp.maximum(1.0-u,0.0)
                w=t_*rcp(s)
                return (w*w)*(w*t_)*((1.25-t_)*j(3))
            def many(k,total):
                t=first+k*JB
                return total+functools.reduce(lambda p,q:p+q,[tile(t+i) for i in range(JB)])
            total=lax.fori_loop(0,nfull,many,jnp.zeros((IB,128),jnp.float32))
            if JB>1:
                total=lax.fori_loop(first+nfull*JB,last,lambda t,tt:tt+tile(t),total)
            acc[a,rows,:]=total
            return 0
        groups=lax.shift_right_logical(count+15,4)
        rest=lax.bitwise_and(groups,3)
        big=lax.shift_right_logical(groups+1,2)
        lax.fori_loop(0,big,lambda g,c:iblock(64,J64,g*64,c),0)
        lax.fori_loop(0,jnp.where(rest==2,1,0),lambda g,c:iblock(32,J32,big*64,c),0)
        lax.fori_loop(0,jnp.where(rest==1,1,0),lambda g,c:iblock(16,J16,big*64,c),0)
        return 0
    lax.fori_loop(0,CELLS,cell,0)
    for a in range(CELLS):
        sums=jnp.sum(acc[a].T,axis=0,keepdims=True)
        there=rec[meta[0,2,a],3:4,:]>0
        rho[a:a+1,:]=jnp.where(there,(32.0*NORM)*sums,0.0)
        safe[a:a+1,:]=jnp.where(there,(32.0*NORM)*sums,1.0)
    leave.wait()

def density(rec,meta,pairs,cols,J64=2,J32=4,J16=4,U=8):
    V=pl.BlockSpec(memory_space=pltpu.VMEM); S=pl.BlockSpec(memory_space=pltpu.SMEM); H=pl.BlockSpec(memory_space=pltpu.HBM)
    return pl.pallas_call(functools.partial(density_kernel,J64,J32,J16,U),
        out_shape=(jax.ShapeDtypeStruct((CELLS,SLOTS),jnp.float32),jax.ShapeDtypeStruct((CELLS,SLOTS),jnp.float32),jax.ShapeDtypeStruct((384,),jnp.int32),jax.ShapeDtypeStruct((MAXT,8,128),jnp.float32)),
        in_specs=[H,H,H,H],out_specs=(V,V,S,H),
        scratch_shapes=[pltpu.VMEM((144,8,SLOTS),jnp.float32),pltpu.SMEM((9,4,128),jnp.int32),pltpu.SMEM((3,NPAIRS),jnp.int32),pltpu.VMEM((MAXT,8,128),jnp.float32),pltpu.SemaphoreType.DMA((4,)),pltpu.SMEM((CELLS,),jnp.int32),pltpu.SMEM((NPAIRS,),jnp.int32),pltpu.SMEM((NPAIRS,),jnp.int32),pltpu.VMEM((27,8,128),jnp.float32),pltpu.VMEM((CELLS,4,SLOTS,128),jnp.float32),pltpu.SemaphoreType.DMA((CELLS,)),pltpu.VMEM((CELLS,SLOTS,128),jnp.float32)],
        compiler_params=pltpu.CompilerParams(vmem_limit_bytes=WHOLE),
        name="density")(rec,meta,pairs,cols)

def force_kernel(J32,J16,U,rec_in,snd_in,rho_in,meta_in,tab_in,buf_in,cols_in,rest_in,out,rec,snd,rho,meta,tab,buf,sems,extra,cells,cols,col_sems,acc):
    copies=fetch(((snd_in,snd),(rho_in,rho),(tab_in,tab),(meta_in.at[0],meta.at[0]),(rec_in.at[pl.ds(0,CELLS)],rec),(buf_in,buf)),sems)
    copies[3].wait()
    def column_copy(a):
        return (pltpu.make_async_copy(cols_in.at[meta[0,2,a]],cols.at[a,pl.ds(0,7)],col_sems.at[0,a]),
                pltpu.make_async_copy(rest_in.at[a],cols.at[a,pl.ds(7,3)],col_sems.at[1,a]))
    def ask(a,_):
        for copy in column_copy(a):
            copy.start()
        return 0
    lax.fori_loop(0,CELLS,ask,0)
    for copy in copies[:3]:
        copy.wait()
    for n in range(9):
        for half in range(2):
            c8=slice(8*half,8*half+8)
            c2=snd[n,c8,:]; rr=rho[n,c8,:]
            base=(n*16+8*half)*8
            for f,val in enumerate(extra_fields(c2,rr)):
                cells[0,pl.ds(base+f,8,stride=8),:]=val[:,0:128]
                cells[1,pl.ds(base+f,8,stride=8),:]=val[:,128:256]
    lane=lax.broadcasted_iota(jnp.int32,(8,128),1)
    block=lambda src: pl.ds(pl.multiple_of(src*8,8),8)
    def put(p,_):
        src=tab[p]
        append(extra,cells[0,block(src),:],cells[1,block(src),:],tab[PLACE+p],lane)
        return 0
    lax.fori_loop(0,NPAIRS,put,0,unroll=U)
    for copy in copies[4:]:
        copy.wait()
    def cell(a,_):
        for copy in column_copy(a):
            copy.wait()
        first=tab[FIRST+a]; last=tab[LAST+a]
        count=meta[0,0,a]
        def iblock(IB,JB,start,_):
            rows=pl.ds(pl.multiple_of(start,16),IB)
            nfull=(last-first)//JB
            def tile(t):
                i=lambda f: cols[a,f,rows,:]
                j=lambda rw: buf[t,rw:rw+1,:]
                e=lambda rw: extra[t,rw:rw+1,:]
                dx=i(0)-j(0); dy=i(1)-j(1); dz=i(2)-j(2)
                r2=dx*dx+dy*dy+dz*dz
                s=i(3)+j(4)
                inv=rcp(s)
                u=rcp(s*lax.rsqrt(r2))
                w=jnp.maximum(1.0-u,0.0)*inv
                va=jnp.minimum((i(4)-j(5))*dx+(i(5)-j(6))*dy+(i(6)-j(7))*dz,0.0)
                m=va*inv*rcp(u*u+0.0025)
                visc=m*((m-i(7))-e(0))*rcp(i(9)+e(2))
                f=(i(8)+e(1)+visc)*j(3)*((w*w)*(w*(inv*inv)))
                return f*dx,f*dy,f*dz
            def many(k,total):
                t=first+k*JB
                ts=[tile(t+q) for q in range(JB)]
                return tuple(total[c]+functools.reduce(lambda p,q:p+q,[x[c] for x in ts]) for c in range(3))
            z=jnp.zeros((IB,128),jnp.float32)
            total=lax.fori_loop(0,nfull,many,(z,z,z))
            if JB>1:
                def one(t,tt):
                    x=tile(t)
                    return tuple(p+q for p,q in zip(tt,x))
                total=lax.fori_loop(first+nfull*JB,last,one,total)
            for c in range(3):
                acc[c,a,rows,:]=total[c]
            return 0
        groups=lax.shift_right_logical(count+15,4)
        big=lax.shift_right_logical(groups,1)
        lax.fori_loop(0,big,lambda g,c:iblock(32,J32,g*32,c),0)
        lax.fori_loop(0,lax.bitwise_and(groups,1),lambda g,c:iblock(16,J16,big*32,c),0)
        return 0
    lax.fori_loop(0,CELLS,cell,0)
    for a in range(CELLS):
        for c in range(3):
            sums=jnp.sum(acc[c,a].T,axis=0,keepdims=True)
            out[c,a:a+1,:]=jnp.where(rec[meta[0,2,a],3:4,:]>0,(160.0*NORM)*sums,0.0)

def force(rec,snd,rho,meta,tab,buf,cols,rest,J32=4,J16=4,U=8):
    V=pl.BlockSpec(memory_space=pltpu.VMEM); S=pl.BlockSpec(memory_space=pltpu.SMEM); H=pl.BlockSpec(memory_space=pltpu.HBM)
    return pl.pallas_call(functools.partial(force_kernel,J32,J16,U),
        out_shape=jax.ShapeDtypeStruct((3,CELLS,SLOTS),jnp.float32),
        in_specs=[H]*8,out_specs=V,
        scratch_shapes=[pltpu.VMEM((CELLS,8,SLOTS),jnp.float32),pltpu.VMEM((9,CELLS,SLOTS),jnp.float32),pltpu.VMEM((9,CELLS,SLOTS),jnp.float32),pltpu.SMEM((1,4,128),jnp.int32),pltpu.SMEM((384,),jnp.int32),pltpu.VMEM((MAXT,8,128),jnp.float32),pltpu.SemaphoreType.DMA((6,)),pltpu.VMEM((MAXT,8,128),jnp.float32),pltpu.VMEM((2,144*8,128),jnp.float32),pltpu.VMEM((CELLS,10,SLOTS,128),jnp.float32),pltpu.SemaphoreType.DMA((2,CELLS)),pltpu.VMEM((3,CELLS,SLOTS,128),jnp.float32)],
        compiler_params=pltpu.CompilerParams(vmem_limit_bytes=WHOLE),
        name="force")(rec,snd,rho,meta,tab,buf,cols,rest)


from jax.sharding import PartitionSpec as P

N_GX=16; N_GY=8
AROUND=((-1,-1),(-1,0),(-1,1),(0,-1),(0,1),(1,-1),(1,0),(1,1))
MESH=pl.DeviceIdType.MESH
OWN_FIELDS=(0, 1, 2, 4, 5, 6, 7)


def neighbours(u, w):
    return [(lax.rem(u + du + N_GX, N_GX), lax.rem(w + dw + N_GY, N_GY)) for du, dw in AROUND]


def exchange_kernel(*refs):
    given, (rec_out, snd_out, meta_out, cols_out), scratch = refs[:8], refs[8:12], refs[12:]
    held, (rec, outbox, inbox, outbox2, inbox2, metas, moved, sounds_moved, cols, load, leave, send1, recv1, send2, recv2) = scratch[:8], scratch[8:]
    pos, vel, mass, smooth, snd, counts, move, lists = held
    u, w = lax.axis_index("gx"), lax.axis_index("gy")
    loads = [pltpu.make_async_copy(src, dst, load.at[k]) for k, (src, dst) in enumerate(zip(given, held))]
    for copy in loads:
        copy.start()
    around = neighbours(u, w)
    barrier = pltpu.get_barrier_semaphore()
    for off in range(1, N_GX):
        pl.semaphore_signal(barrier, inc=1, device_id=(lax.rem(u + off, N_GX), w), device_id_type=MESH)
    for n in (3, 4):
        pl.semaphore_signal(barrier, inc=1, device_id=around[n], device_id_type=MESH)

    for copy in loads:
        copy.wait()
    slot = lax.broadcasted_iota(jnp.int32, (1, 256), 1)
    for c in range(16):
        for f in range(3):
            rec[c, f:f + 1, :] = pos[f, c:c + 1, :]
            rec[c, 5 + f:6 + f, :] = vel[f, c:c + 1, :]
        rec[c, 3:4, :] = jnp.where(slot < counts[c], mass[c:c + 1, :], 0.0)
        rec[c, 4:5, :] = smooth[c:c + 1, :]

    headed = [lax.shift_right_logical(move[c], 7) for c in range(16)]
    row = lax.broadcasted_iota(jnp.int32, (8, 256), 0)

    def post(off, _):
        column = lax.rem(u + off, N_GX)
        first, last = jnp.int32(16), jnp.int32(-1)
        for c in range(16):
            match = headed[c] == column
            first = jnp.minimum(first, jnp.where(match, c, 16))
            last = jnp.where(match, c, last)
        found = last >= 0
        first = jnp.where(found, first, 0)
        last = jnp.where(found, last, 0)
        outbox[off, 0:8, :] = rec[first]
        outbox2[off] = rec[last]
        number = lambda c: jnp.where(found, move[c], -1).astype(jnp.float32)
        amount = lambda c: counts[c].astype(jnp.float32)
        more = jnp.where(row == 0, snd[pl.ds(first, 1), :], snd[pl.ds(last, 1), :])
        more = jnp.where(row == 2, number(first), more)
        more = jnp.where(row == 3, number(last), more)
        more = jnp.where(row == 4, amount(first), more)
        more = jnp.where(row == 5, amount(last), more)
        outbox[off, 8:16, :] = more
        return 0

    lax.fori_loop(0, N_GX, post, 0)
    pl.semaphore_wait(barrier, N_GX - 1 + 2)

    def parcel(off, part):
        src, dst = ((outbox, inbox), (outbox2, inbox2))[part]
        return pltpu.make_async_remote_copy(
            src_ref=src.at[off], dst_ref=dst.at[off], send_sem=send1.at[part, off], recv_sem=recv1.at[part, off],
            device_id=(lax.rem(u + off, N_GX), w), device_id_type=MESH)

    for part in range(2):
        def start(off, _):
            parcel(off, part).start()
            return 0

        lax.fori_loop(1, N_GX, start, 0)
    inbox[0] = outbox[0]
    inbox2[0] = outbox2[0]

    first_own = ((u * N_GY + w) * 16).astype(jnp.float32)
    sub = lax.broadcasted_iota(jnp.int32, (16, 256), 0).astype(jnp.float32) + first_own
    lane = lax.broadcasted_iota(jnp.int32, (1, 128), 1).astype(jnp.float32) + first_own

    def place(cells, block, number, rank):
        key = jnp.broadcast_to(jnp.where(number >= 0.0, rank, -1.0), (8, 256))
        cells = tuple(jnp.where(key == float(k), block, cells[k]) for k in range(8))
        return cells, rank + jnp.where(number >= 0.0, 1.0, 0.0)

    def absorb(off, carry):
        cells, rank, sounds, amounts, ranks = carry
        for k in range(2):
            number = inbox[off, 10 + k:11 + k, :]
            mine = lane == number[:, 0:128]
            sounds = jnp.where(sub == number, inbox[off, 8 + k:9 + k, :], sounds)
            amounts = jnp.where(mine, inbox[off, 12 + k:13 + k, 0:128], amounts)
            ranks = jnp.where(mine, rank[:, 0:128] + 8.0 * k, ranks)
        cells, rank = place(cells, inbox[off, 0:8, :], inbox[off, 10:11, :], rank)
        return cells, rank, sounds, amounts, ranks

    def absorb_next(off, carry):
        parcel(off, 0).wait_recv()
        return absorb(off, carry)

    def absorb2(off, carry):
        return place(carry[0], inbox2[off], inbox[off, 10:11, :], carry[1])

    def absorb2_next(off, carry):
        parcel(off, 1).wait_recv()
        return absorb2(off, carry)

    zero = jnp.zeros((8, 256), jnp.float32)
    line = jnp.zeros((1, 128), jnp.float32)
    none = ((zero,) * 8, jnp.zeros((1, 256), jnp.float32))
    carry = absorb(0, none + (jnp.zeros((16, 256), jnp.float32), line, line))
    cells, _, sounds, amounts, ranks = lax.fori_loop(1, N_GX, absorb_next, carry)
    for k in range(8):
        moved[k] = cells[k]
    sounds_moved[...] = sounds
    metas[0:1, :] = amounts.astype(jnp.int32)
    metas[1:2, :] = lists[...]
    metas[2:3, :] = ranks.astype(jnp.int32)
    metas[3:4, :] = lists[...]

    halves = (pl.ds(0, 8), pl.ds(8, 8))
    own = (metas, moved.at[halves[0]], sounds_moved, moved.at[halves[1]])
    at = lambda n: (meta_out.at[n], rec_out.at[n, halves[0]], snd_out.at[n], rec_out.at[n, halves[1]])
    remote = lambda src, n, k, device: pltpu.make_async_remote_copy(
        src_ref=src, dst_ref=at(n + 1)[k], send_sem=send2.at[n, k], recv_sem=recv2.at[n, k],
        device_id=device, device_id_type=MESH)
    copies, arriving = [], {}

    def spread_out(items):
        for nearest in ((1, 6), (3, 4)):
            for k in items:
                for n in nearest:
                    copy = remote(own[k], n, k, around[n])
                    copy.start()
                    if nearest == (1, 6):
                        arriving[n, k] = copy
                    else:
                        copies.append(copy)

    def pass_on(items):
        for k in items:
            for n in (1, 6):
                arriving[n, k].wait_recv()
                for to, step in ((n - 1, 3), (n + 1, 4)):
                    copy = remote(at(n + 1)[k], to, k, around[step])
                    copy.start()
                    copies.append(copy)

    def column_copy(k):
        return pltpu.make_async_copy(cols.at[k], cols_out.at[k], leave.at[k])

    def make_columns(k, _):
        columns(cols.at[k], moved[k], OWN_FIELDS)
        column_copy(k).start()
        return 0

    spread_out((0, 1, 2))
    cells, _ = lax.fori_loop(1, N_GX, absorb2_next, absorb2(0, none))
    for k in range(8):
        moved[8 + k] = cells[k]
    spread_out((3,))
    for k in range(4):
        copy = pltpu.make_async_copy(own[k], at(0)[k], load.at[k])
        copy.start()
        copies.append(copy)
    pass_on((0, 1, 2, 3))
    lax.fori_loop(0, 16, make_columns, 0)
    for copy in arriving.values():
        copy.wait_send()

    def left(k, _):
        column_copy(k).wait()
        return 0

    lax.fori_loop(0, 16, left, 0)

    def sent(off, _):
        parcel(off, 0).wait_send()
        parcel(off, 1).wait_send()
        return 0

    lax.fori_loop(1, N_GX, sent, 0)
    for copy in copies:
        copy.wait()


VMEM=pl.BlockSpec(memory_space=pltpu.VMEM)
HBM=pl.BlockSpec(memory_space=pltpu.HBM)

def exchange(positions, velocities, masses, smoothing, sound2, counts, move_to, lists):
    return pl.pallas_call(
        exchange_kernel,
        out_shape=(jax.ShapeDtypeStruct((9, 16, 8, 256), jnp.float32),
                   jax.ShapeDtypeStruct((9, 16, 256), jnp.float32),
                   jax.ShapeDtypeStruct((9, 4, 128), jnp.int32),
                   jax.ShapeDtypeStruct((16, 7, 256, 128), jnp.float32)),
        in_specs=[HBM] * 8,
        out_specs=(HBM,) * 4,
        scratch_shapes=[
            pltpu.VMEM((3, 16, 256), jnp.float32),
            pltpu.VMEM((3, 16, 256), jnp.float32),
            pltpu.VMEM((16, 256), jnp.float32),
            pltpu.VMEM((16, 256), jnp.float32),
            pltpu.VMEM((16, 256), jnp.float32),
            pltpu.SMEM((16,), jnp.int32),
            pltpu.SMEM((16,), jnp.int32),
            pltpu.VMEM((1, 128), jnp.int32),
            pltpu.VMEM((16, 8, 256), jnp.float32),
            pltpu.VMEM((N_GX, 16, 256), jnp.float32),
            pltpu.VMEM((N_GX, 16, 256), jnp.float32),
            pltpu.VMEM((N_GX, 8, 256), jnp.float32),
            pltpu.VMEM((N_GX, 8, 256), jnp.float32),
            pltpu.VMEM((4, 128), jnp.int32),
            pltpu.VMEM((16, 8, 256), jnp.float32),
            pltpu.VMEM((16, 256), jnp.float32),
            pltpu.VMEM((16, 7, 256, 128), jnp.float32),
            pltpu.SemaphoreType.DMA((8,)),
            pltpu.SemaphoreType.DMA((16,)),
            pltpu.SemaphoreType.DMA((2, N_GX)),
            pltpu.SemaphoreType.DMA((2, N_GX)),
            pltpu.SemaphoreType.DMA((8, 4)),
            pltpu.SemaphoreType.DMA((8, 4)),
        ],
        compiler_params=pltpu.CompilerParams(collective_id=0, has_side_effects=True, vmem_limit_bytes=WHOLE),
        name="exchange",
    )(positions, velocities, masses, smoothing, sound2, counts, move_to, lists)


def share_kernel(own, snd, out, rest_out, own_here, snd_here, rest, load, leave, send, recv):
    u, w = lax.axis_index("gx"), lax.axis_index("gy")
    around = neighbours(u, w)
    barrier = pltpu.get_barrier_semaphore()
    for n in range(8):
        pl.semaphore_signal(barrier, inc=1, device_id=around[n], device_id_type=MESH)
    loads = [pltpu.make_async_copy(own, own_here, load.at[0]), pltpu.make_async_copy(snd.at[0], snd_here, load.at[1])]
    copies = [pltpu.make_async_copy(own, out.at[0], load.at[2])]
    for copy in loads + copies:
        copy.start()
    pl.semaphore_wait(barrier, 8)
    for n in range(8):
        copy = pltpu.make_async_remote_copy(
            src_ref=own, dst_ref=out.at[n + 1], send_sem=send.at[n], recv_sem=recv.at[n],
            device_id=around[n], device_id_type=MESH)
        copy.start()
        copies.append(copy)
    for copy in loads:
        copy.wait()
    fields = extra_fields(snd_here[...], own_here[...])
    for a in range(16):
        columns(rest.at[a], jnp.concatenate([field[a:a + 1] for field in fields], 0), (0, 1, 2))
        copy = pltpu.make_async_copy(rest.at[a], rest_out.at[a], leave.at[a])
        copy.start()
        copies.append(copy)
    for copy in copies:
        copy.wait()


def share(own, snd):
    return pl.pallas_call(
        share_kernel,
        out_shape=(jax.ShapeDtypeStruct((9, 16, 256), jnp.float32), jax.ShapeDtypeStruct((16, 3, 256, 128), jnp.float32)),
        in_specs=[HBM] * 2, out_specs=(HBM,) * 2,
        scratch_shapes=[
            pltpu.VMEM((16, 256), jnp.float32),
            pltpu.VMEM((16, 256), jnp.float32),
            pltpu.VMEM((16, 3, 256, 128), jnp.float32),
            pltpu.SemaphoreType.DMA((3,)),
            pltpu.SemaphoreType.DMA((16,)),
            pltpu.SemaphoreType.DMA((8,)),
            pltpu.SemaphoreType.DMA((8,)),
        ],
        compiler_params=pltpu.CompilerParams(collective_id=1, has_side_effects=True, vmem_limit_bytes=WHOLE),
        name="share",
    )(own, snd)


def body(positions, velocities, masses, smoothing, sound2, counts, move_to, proxy_send, pairs):
    rec, snd, meta, cols = exchange(positions, velocities, masses, smoothing, sound2, counts, move_to, proxy_send.reshape(1, 128))
    rec = rec.reshape(144, 8, 256)
    rho, safe, tab, buf = density(rec, meta, pairs.T, cols)
    rho_all, rest = share(safe, snd)
    accel = force(rec, snd, rho_all, meta, tab, buf, cols, rest)
    return rho, accel


def solution(mesh):
    flat, cells, three = P(("gx", "gy")), P(("gx", "gy"), None), P(None, ("gx", "gy"), None)
    return jax.shard_map(
        body, mesh=mesh,
        in_specs=(three, three, cells, cells, cells, flat, flat, flat, cells),
        out_specs=(cells, three), check_vma=False)
```

```python
import math, functools
import jax, jax.numpy as jnp
from jax import lax
from jax.experimental import pallas as pl
from jax.experimental.pallas import tpu as pltpu

CELLS=16; SLOTS=256; NPAIRS=160; NORM=21.0/(16.0*math.pi)
WHOLE=63<<20
MAXT=2*NPAIRS+3*CELLS+8
PLACE=NPAIRS; FIRST=2*NPAIRS; LAST=FIRST+CELLS

def rcp(x):
    return pl.reciprocal(x, approx=True)

def append(buf, x0, x1, pos, lane):
    tile=lax.shift_right_logical(pos,7); s=lax.bitwise_and(pos,127)
    t0=pltpu.roll(x0,s,1); t1=pltpu.roll(x1,s,1)
    keep=lane>=s
    pltpu.store(buf.at[tile],t0,mask=keep)
    buf[tile+1]=jnp.where(keep,t1,t0)
    buf[tile+2]=jnp.where(keep,0.0,t1)

def plan(meta, pairs, tab, filled, count_of, place_of):
    for a in range(CELLS):
        filled[a]=0
    def size(p,_):
        a=pairs[0,p]; b=pairs[1,p]
        n=lax.shift_right_logical(b,4); r=lax.bitwise_and(b,15)
        cell=jnp.where(n==0,r,meta[n,1,jnp.maximum(n-1,0)*16+r])
        count=meta[n,0,cell]
        tab[p]=n*16+cell
        place_of[p]=n*16+meta[n,2,cell]
        count_of[p]=count
        filled[a]=filled[a]+count
        return 0
    lax.fori_loop(0,NPAIRS,size,0,unroll=8)
    tile=jnp.int32(0)
    for a in range(CELLS):
        end=tile+lax.shift_right_logical(filled[a]+127,7)
        tab[FIRST+a]=tile; tab[LAST+a]=end
        filled[a]=tile*128
        tile=end+2

def pack_main(rec, pairs, tab, filled, count_of, place_of, shifts, buf, unroll):
    lane=lax.broadcasted_iota(jnp.int32,(8,128),1)
    row=lax.broadcasted_iota(jnp.int32,(8,128),0)
    for d in range(27):
        dx,dy,dz=d//9-1,d//3%3-1,d%3-1
        shifts[d]=jnp.where(row==0,float(dx),jnp.where(row==1,float(dy),jnp.where(row==2,float(dz),0.0)))
    def put(p,_):
        a=pairs[0,p]
        pos=filled[a]
        filled[a]=pos+count_of[p]
        tab[PLACE+p]=pos
        src=place_of[p]; shift=shifts[pairs[2,p]]
        append(buf,rec[src,:,0:128]+shift,rec[src,:,128:256]+shift,pos,lane)
        return 0
    lax.fori_loop(0,NPAIRS,put,0,unroll=unroll)

def columns(icol, block, rows):
    for f,row in enumerate(rows):
        for half in range(2):
            lanes=slice(128*half,128*half+128)
            icol[f,lanes,:]=jnp.broadcast_to(block[row:row+1,lanes],(128,128)).T

def extra_fields(c2, rho):
    return 0.5*(c2*lax.rsqrt(c2)),c2*rcp(rho),rho

def fetch(pairs_of_refs, sems):
    copies=[pltpu.make_async_copy(src,dst,sems.at[k]) for k,(src,dst) in enumerate(pairs_of_refs)]
    for copy in copies:
        copy.start()
    return copies

def density_kernel(J64,J32,J16,U,rec_in,meta_in,pairs_in,cols_in,rho,safe,tab,buf_out,rec,meta,pairs,buf,sems,filled,count_of,place_of,shifts,cols,col_sems,acc):
    copies=fetch(((meta_in,meta),(pairs_in,pairs),(rec_in,rec)),sems)
    copies[0].wait(); copies[1].wait()
    def column_copy(a):
        return pltpu.make_async_copy(cols_in.at[meta[0,2,a],pl.ds(0,4)],cols.at[a],col_sems.at[a])
    def ask(a,_):
        column_copy(a).start()
        return 0
    lax.fori_loop(0,CELLS,ask,0)
    plan(meta,pairs,tab,filled,count_of,place_of)
    copies[2].wait()
    pack_main(rec,pairs,tab,filled,count_of,place_of,shifts,buf,U)
    leave=pltpu.make_async_copy(buf,buf_out,sems.at[3])
    leave.start()
    def cell(a,_):
        column_copy(a).wait()
        icol=cols.at[a]
        first=tab[FIRST+a]; last=tab[LAST+a]
        count=meta[0,0,a]
        def iblock(IB,JB,start,_):
            rows=pl.ds(pl.multiple_of(start,16),IB)
            nfull=(last-first)//JB
            xi,yi,zi,hi=(icol[f,rows,:] for f in range(4))
            def tile(t):
                j=lambda rw: buf[t,rw:rw+1,:]
                dx=xi-j(0); dy=yi-j(1); dz=zi-j(2)
                r2=dx*dx+dy*dy+dz*dz
                s=hi+j(4)
                u=rcp(s*lax.rsqrt(r2))
                t_=jnp.maximum(1.0-u,0.0)
                w=t_*rcp(s)
                return (w*w)*(w*t_)*((1.25-t_)*j(3))
            def many(k,total):
                t=first+k*JB
                return total+functools.reduce(lambda p,q:p+q,[tile(t+i) for i in range(JB)])
            total=lax.fori_loop(0,nfull,many,jnp.zeros((IB,128),jnp.float32))
            if JB>1:
                total=lax.fori_loop(first+nfull*JB,last,lambda t,tt:tt+tile(t),total)
            acc[a,rows,:]=total
            return 0
        groups=lax.shift_right_logical(count+15,4)
        rest=lax.bitwise_and(groups,3)
        big=lax.shift_right_logical(groups+1,2)
        lax.fori_loop(0,big,lambda g,c:iblock(64,J64,g*64,c),0)
        lax.fori_loop(0,jnp.where(rest==2,1,0),lambda g,c:iblock(32,J32,big*64,c),0)
        lax.fori_loop(0,jnp.where(rest==1,1,0),lambda g,c:iblock(16,J16,big*64,c),0)
        return 0
    lax.fori_loop(0,CELLS,cell,0)
    for a in range(CELLS):
        sums=jnp.sum(acc[a].T,axis=0,keepdims=True)
        there=rec[meta[0,2,a],3:4,:]>0
        rho[a:a+1,:]=jnp.where(there,(32.0*NORM)*sums,0.0)
        safe[a:a+1,:]=jnp.where(there,(32.0*NORM)*sums,1.0)
    leave.wait()

def density(rec,meta,pairs,cols,J64=2,J32=4,J16=4,U=8):
    V=pl.BlockSpec(memory_space=pltpu.VMEM); S=pl.BlockSpec(memory_space=pltpu.SMEM); H=pl.BlockSpec(memory_space=pltpu.HBM)
    return pl.pallas_call(functools.partial(density_kernel,J64,J32,J16,U),
        out_shape=(jax.ShapeDtypeStruct((CELLS,SLOTS),jnp.float32),jax.ShapeDtypeStruct((CELLS,SLOTS),jnp.float32),jax.ShapeDtypeStruct((384,),jnp.int32),jax.ShapeDtypeStruct((MAXT,8,128),jnp.float32)),
        in_specs=[H,H,H,H],out_specs=(V,V,S,H),
        scratch_shapes=[pltpu.VMEM((144,8,SLOTS),jnp.float32),pltpu.SMEM((9,4,128),jnp.int32),pltpu.SMEM((3,NPAIRS),jnp.int32),pltpu.VMEM((MAXT,8,128),jnp.float32),pltpu.SemaphoreType.DMA((4,)),pltpu.SMEM((CELLS,),jnp.int32),pltpu.SMEM((NPAIRS,),jnp.int32),pltpu.SMEM((NPAIRS,),jnp.int32),pltpu.VMEM((27,8,128),jnp.float32),pltpu.VMEM((CELLS,4,SLOTS,128),jnp.float32),pltpu.SemaphoreType.DMA((CELLS,)),pltpu.VMEM((CELLS,SLOTS,128),jnp.float32)],
        compiler_params=pltpu.CompilerParams(vmem_limit_bytes=WHOLE),
        name="density")(rec,meta,pairs,cols)

def force_kernel(J32,J16,U,rec_in,snd_in,rho_in,meta_in,tab_in,buf_in,cols_in,rest_in,out,rec,snd,rho,meta,tab,buf,sems,extra,cells,cols,col_sems,acc):
    copies=fetch(((snd_in,snd),(rho_in,rho),(tab_in,tab),(meta_in.at[0],meta.at[0]),(rec_in.at[pl.ds(0,CELLS)],rec),(buf_in,buf)),sems)
    copies[3].wait()
    def column_copy(a):
        return (pltpu.make_async_copy(cols_in.at[meta[0,2,a]],cols.at[a,pl.ds(0,7)],col_sems.at[0,a]),
                pltpu.make_async_copy(rest_in.at[a],cols.at[a,pl.ds(7,3)],col_sems.at[1,a]))
    def ask(a,_):
        for copy in column_copy(a):
            copy.start()
        return 0
    lax.fori_loop(0,CELLS,ask,0)
    for copy in copies[:3]:
        copy.wait()
    for n in range(9):
        for half in range(2):
            c8=slice(8*half,8*half+8)
            c2=snd[n,c8,:]; rr=rho[n,c8,:]
            base=(n*16+8*half)*8
            for f,val in enumerate(extra_fields(c2,rr)):
                cells[0,pl.ds(base+f,8,stride=8),:]=val[:,0:128]
                cells[1,pl.ds(base+f,8,stride=8),:]=val[:,128:256]
    lane=lax.broadcasted_iota(jnp.int32,(8,128),1)
    block=lambda src: pl.ds(pl.multiple_of(src*8,8),8)
    def put(p,_):
        src=tab[p]
        append(extra,cells[0,block(src),:],cells[1,block(src),:],tab[PLACE+p],lane)
        return 0
    lax.fori_loop(0,NPAIRS,put,0,unroll=U)
    for copy in copies[4:]:
        copy.wait()
    def cell(a,_):
        for copy in column_copy(a):
            copy.wait()
        first=tab[FIRST+a]; last=tab[LAST+a]
        count=meta[0,0,a]
        def iblock(IB,JB,start,_):
            rows=pl.ds(pl.multiple_of(start,16),IB)
            nfull=(last-first)//JB
            def tile(t):
                i=lambda f: cols[a,f,rows,:]
                j=lambda rw: buf[t,rw:rw+1,:]
                e=lambda rw: extra[t,rw:rw+1,:]
                dx=i(0)-j(0); dy=i(1)-j(1); dz=i(2)-j(2)
                r2=dx*dx+dy*dy+dz*dz
                s=i(3)+j(4)
                inv=rcp(s)
                u=rcp(s*lax.rsqrt(r2))
                w=jnp.maximum(1.0-u,0.0)*inv
                va=jnp.minimum((i(4)-j(5))*dx+(i(5)-j(6))*dy+(i(6)-j(7))*dz,0.0)
                m=va*inv*rcp(u*u+0.0025)
                visc=m*((m-i(7))-e(0))*rcp(i(9)+e(2))
                f=(i(8)+e(1)+visc)*j(3)*((w*w)*(w*(inv*inv)))
                return f*dx,f*dy,f*dz
            def many(k,total):
                t=first+k*JB
                ts=[tile(t+q) for q in range(JB)]
                return tuple(total[c]+functools.reduce(lambda p,q:p+q,[x[c] for x in ts]) for c in range(3))
            z=jnp.zeros((IB,128),jnp.float32)
            total=lax.fori_loop(0,nfull,many,(z,z,z))
            if JB>1:
                def one(t,tt):
                    x=tile(t)
                    return tuple(p+q for p,q in zip(tt,x))
                total=lax.fori_loop(first+nfull*JB,last,one,total)
            for c in range(3):
                acc[c,a,rows,:]=total[c]
            return 0
        groups=lax.shift_right_logical(count+15,4)
        big=lax.shift_right_logical(groups,1)
        lax.fori_loop(0,big,lambda g,c:iblock(32,J32,g*32,c),0)
        lax.fori_loop(0,lax.bitwise_and(groups,1),lambda g,c:iblock(16,J16,big*32,c),0)
        return 0
    lax.fori_loop(0,CELLS,cell,0)
    for a in range(CELLS):
        for c in range(3):
            sums=jnp.sum(acc[c,a].T,axis=0,keepdims=True)
            out[c,a:a+1,:]=jnp.where(rec[meta[0,2,a],3:4,:]>0,(160.0*NORM)*sums,0.0)

def force(rec,snd,rho,meta,tab,buf,cols,rest,J32=4,J16=4,U=16):
    V=pl.BlockSpec(memory_space=pltpu.VMEM); S=pl.BlockSpec(memory_space=pltpu.SMEM); H=pl.BlockSpec(memory_space=pltpu.HBM)
    return pl.pallas_call(functools.partial(force_kernel,J32,J16,U),
        out_shape=jax.ShapeDtypeStruct((3,CELLS,SLOTS),jnp.float32),
        in_specs=[H]*8,out_specs=V,
        scratch_shapes=[pltpu.VMEM((CELLS,8,SLOTS),jnp.float32),pltpu.VMEM((9,CELLS,SLOTS),jnp.float32),pltpu.VMEM((9,CELLS,SLOTS),jnp.float32),pltpu.SMEM((1,4,128),jnp.int32),pltpu.SMEM((384,),jnp.int32),pltpu.VMEM((MAXT,8,128),jnp.float32),pltpu.SemaphoreType.DMA((6,)),pltpu.VMEM((MAXT,8,128),jnp.float32),pltpu.VMEM((2,144*8,128),jnp.float32),pltpu.VMEM((CELLS,10,SLOTS,128),jnp.float32),pltpu.SemaphoreType.DMA((2,CELLS)),pltpu.VMEM((3,CELLS,SLOTS,128),jnp.float32)],
        compiler_params=pltpu.CompilerParams(vmem_limit_bytes=WHOLE),
        name="force")(rec,snd,rho,meta,tab,buf,cols,rest)


from jax.sharding import PartitionSpec as P

N_GX=16; N_GY=8
AROUND=((-1,-1),(-1,0),(-1,1),(0,-1),(0,1),(1,-1),(1,0),(1,1))
MESH=pl.DeviceIdType.MESH
FAR_FIRST=(6, 10, 7, 9, 2, 14, 5, 11, 8, 3, 13, 1, 15, 4, 12)
OWN_FIELDS=(0, 1, 2, 4, 5, 6, 7)


def neighbours(u, w):
    return [(lax.rem(u + du + N_GX, N_GX), lax.rem(w + dw + N_GY, N_GY)) for du, dw in AROUND]


def exchange_kernel(*refs):
    given, (rec_out, snd_out, meta_out, cols_out), scratch = refs[:8], refs[8:12], refs[12:]
    held, (rec, outbox, inbox, outbox2, inbox2, metas, moved, sounds_moved, cols, load, leave, send1, recv1, send2, recv2) = scratch[:8], scratch[8:]
    pos, vel, mass, smooth, snd, counts, move, lists = held
    u, w = lax.axis_index("gx"), lax.axis_index("gy")
    loads = [pltpu.make_async_copy(src, dst, load.at[k]) for k, (src, dst) in enumerate(zip(given, held))]
    for copy in loads:
        copy.start()
    around = neighbours(u, w)
    barrier = pltpu.get_barrier_semaphore()
    for off in range(1, N_GX):
        pl.semaphore_signal(barrier, inc=1, device_id=(lax.rem(u + off, N_GX), w), device_id_type=MESH)
    for n in (3, 4):
        pl.semaphore_signal(barrier, inc=1, device_id=around[n], device_id_type=MESH)

    for copy in loads:
        copy.wait()
    slot = lax.broadcasted_iota(jnp.int32, (1, 256), 1)
    for c in range(16):
        for f in range(3):
            rec[c, f:f + 1, :] = pos[f, c:c + 1, :]
            rec[c, 5 + f:6 + f, :] = vel[f, c:c + 1, :]
        rec[c, 3:4, :] = jnp.where(slot < counts[c], mass[c:c + 1, :], 0.0)
        rec[c, 4:5, :] = smooth[c:c + 1, :]

    headed = [lax.shift_right_logical(move[c], 7) for c in range(16)]
    row = lax.broadcasted_iota(jnp.int32, (8, 256), 0)

    def post(off, _):
        column = lax.rem(u + off, N_GX)
        first, last = jnp.int32(16), jnp.int32(-1)
        for c in range(16):
            match = headed[c] == column
            first = jnp.minimum(first, jnp.where(match, c, 16))
            last = jnp.where(match, c, last)
        found = last >= 0
        first = jnp.where(found, first, 0)
        last = jnp.where(found, last, 0)
        outbox[off, 0:8, :] = rec[first]
        outbox2[off] = rec[last]
        number = lambda c: jnp.where(found, move[c], -1).astype(jnp.float32)
        amount = lambda c: counts[c].astype(jnp.float32)
        more = jnp.where(row == 0, snd[pl.ds(first, 1), :], snd[pl.ds(last, 1), :])
        more = jnp.where(row == 2, number(first), more)
        more = jnp.where(row == 3, number(last), more)
        more = jnp.where(row == 4, amount(first), more)
        more = jnp.where(row == 5, amount(last), more)
        outbox[off, 8:16, :] = more
        return 0

    lax.fori_loop(0, N_GX, post, 0)
    pl.semaphore_wait(barrier, N_GX - 1 + 2)

    def parcel(off, part):
        src, dst = ((outbox, inbox), (outbox2, inbox2))[part]
        return pltpu.make_async_remote_copy(
            src_ref=src.at[off], dst_ref=dst.at[off], send_sem=send1.at[part, off], recv_sem=recv1.at[part, off],
            device_id=(lax.rem(u + off, N_GX), w), device_id_type=MESH)

    for part in range(2):
        for off in FAR_FIRST:
            parcel(off, part).start()
    inbox[0] = outbox[0]
    inbox2[0] = outbox2[0]

    first_own = ((u * N_GY + w) * 16).astype(jnp.float32)
    sub = lax.broadcasted_iota(jnp.int32, (16, 256), 0).astype(jnp.float32) + first_own
    lane = lax.broadcasted_iota(jnp.int32, (1, 128), 1).astype(jnp.float32) + first_own

    def place(cells, block, number, rank):
        key = jnp.broadcast_to(jnp.where(number >= 0.0, rank, -1.0), (8, 256))
        cells = tuple(jnp.where(key == float(k), block, cells[k]) for k in range(8))
        return cells, rank + jnp.where(number >= 0.0, 1.0, 0.0)

    def absorb(off, carry):
        cells, rank, sounds, amounts, ranks = carry
        for k in range(2):
            number = inbox[off, 10 + k:11 + k, :]
            mine = lane == number[:, 0:128]
            sounds = jnp.where(sub == number, inbox[off, 8 + k:9 + k, :], sounds)
            amounts = jnp.where(mine, inbox[off, 12 + k:13 + k, 0:128], amounts)
            ranks = jnp.where(mine, rank[:, 0:128] + 8.0 * k, ranks)
        cells, rank = place(cells, inbox[off, 0:8, :], inbox[off, 10:11, :], rank)
        return cells, rank, sounds, amounts, ranks

    def absorb_next(off, carry):
        parcel(off, 0).wait_recv()
        return absorb(off, carry)

    def absorb2(off, carry):
        return place(carry[0], inbox2[off], inbox[off, 10:11, :], carry[1])

    def absorb2_next(off, carry):
        parcel(off, 1).wait_recv()
        return absorb2(off, carry)

    zero = jnp.zeros((8, 256), jnp.float32)
    line = jnp.zeros((1, 128), jnp.float32)
    none = ((zero,) * 8, jnp.zeros((1, 256), jnp.float32))
    carry = absorb(0, none + (jnp.zeros((16, 256), jnp.float32), line, line))
    cells, _, sounds, amounts, ranks = lax.fori_loop(1, N_GX, absorb_next, carry)
    for k in range(8):
        moved[k] = cells[k]
    sounds_moved[...] = sounds
    metas[0:1, :] = amounts.astype(jnp.int32)
    metas[1:2, :] = lists[...]
    metas[2:3, :] = ranks.astype(jnp.int32)
    metas[3:4, :] = lists[...]

    halves = (pl.ds(0, 8), pl.ds(8, 8))
    own = (metas, moved.at[halves[0]], sounds_moved, moved.at[halves[1]])
    at = lambda n: (meta_out.at[n], rec_out.at[n, halves[0]], snd_out.at[n], rec_out.at[n, halves[1]])
    remote = lambda src, n, k, device: pltpu.make_async_remote_copy(
        src_ref=src, dst_ref=at(n + 1)[k], send_sem=send2.at[n, k], recv_sem=recv2.at[n, k],
        device_id=device, device_id_type=MESH)
    copies, arriving = [], {}

    def spread_out(items):
        for nearest in ((1, 6), (3, 4)):
            for k in items:
                for n in nearest:
                    copy = remote(own[k], n, k, around[n])
                    copy.start()
                    if nearest == (1, 6):
                        arriving[n, k] = copy
                    else:
                        copies.append(copy)

    def pass_on(items):
        for k in items:
            for n in (1, 6):
                arriving[n, k].wait_recv()
                for to, step in ((n - 1, 3), (n + 1, 4)):
                    copy = remote(at(n + 1)[k], to, k, around[step])
                    copy.start()
                    copies.append(copy)

    def column_copy(k):
        return pltpu.make_async_copy(cols.at[k], cols_out.at[k], leave.at[k])

    def make_columns(k, _):
        columns(cols.at[k], moved[k], OWN_FIELDS)
        column_copy(k).start()
        return 0

    spread_out((0, 1, 2))
    cells, _ = lax.fori_loop(1, N_GX, absorb2_next, absorb2(0, none))
    for k in range(8):
        moved[8 + k] = cells[k]
    spread_out((3,))
    for k in range(4):
        copy = pltpu.make_async_copy(own[k], at(0)[k], load.at[k])
        copy.start()
        copies.append(copy)
    pass_on((0, 1, 2, 3))
    lax.fori_loop(0, 16, make_columns, 0)
    for copy in arriving.values():
        copy.wait_send()

    def left(k, _):
        column_copy(k).wait()
        return 0

    lax.fori_loop(0, 16, left, 0)

    def sent(off, _):
        parcel(off, 0).wait_send()
        parcel(off, 1).wait_send()
        return 0

    lax.fori_loop(1, N_GX, sent, 0)
    for copy in copies:
        copy.wait()


VMEM=pl.BlockSpec(memory_space=pltpu.VMEM)
HBM=pl.BlockSpec(memory_space=pltpu.HBM)

def exchange(positions, velocities, masses, smoothing, sound2, counts, move_to, lists):
    return pl.pallas_call(
        exchange_kernel,
        out_shape=(jax.ShapeDtypeStruct((9, 16, 8, 256), jnp.float32),
                   jax.ShapeDtypeStruct((9, 16, 256), jnp.float32),
                   jax.ShapeDtypeStruct((9, 4, 128), jnp.int32),
                   jax.ShapeDtypeStruct((16, 7, 256, 128), jnp.float32)),
        in_specs=[HBM] * 8,
        out_specs=(HBM,) * 4,
        scratch_shapes=[
            pltpu.VMEM((3, 16, 256), jnp.float32),
            pltpu.VMEM((3, 16, 256), jnp.float32),
            pltpu.VMEM((16, 256), jnp.float32),
            pltpu.VMEM((16, 256), jnp.float32),
            pltpu.VMEM((16, 256), jnp.float32),
            pltpu.SMEM((16,), jnp.int32),
            pltpu.SMEM((16,), jnp.int32),
            pltpu.VMEM((1, 128), jnp.int32),
            pltpu.VMEM((16, 8, 256), jnp.float32),
            pltpu.VMEM((N_GX, 16, 256), jnp.float32),
            pltpu.VMEM((N_GX, 16, 256), jnp.float32),
            pltpu.VMEM((N_GX, 8, 256), jnp.float32),
            pltpu.VMEM((N_GX, 8, 256), jnp.float32),
            pltpu.VMEM((4, 128), jnp.int32),
            pltpu.VMEM((16, 8, 256), jnp.float32),
            pltpu.VMEM((16, 256), jnp.float32),
            pltpu.VMEM((16, 7, 256, 128), jnp.float32),
            pltpu.SemaphoreType.DMA((8,)),
            pltpu.SemaphoreType.DMA((16,)),
            pltpu.SemaphoreType.DMA((2, N_GX)),
            pltpu.SemaphoreType.DMA((2, N_GX)),
            pltpu.SemaphoreType.DMA((8, 4)),
            pltpu.SemaphoreType.DMA((8, 4)),
        ],
        compiler_params=pltpu.CompilerParams(collective_id=0, has_side_effects=True, vmem_limit_bytes=WHOLE),
        name="exchange",
    )(positions, velocities, masses, smoothing, sound2, counts, move_to, lists)


def share_kernel(own, snd, out, rest_out, own_here, snd_here, rest, load, leave, send, recv):
    u, w = lax.axis_index("gx"), lax.axis_index("gy")
    around = neighbours(u, w)
    barrier = pltpu.get_barrier_semaphore()
    for n in range(8):
        pl.semaphore_signal(barrier, inc=1, device_id=around[n], device_id_type=MESH)
    loads = [pltpu.make_async_copy(own, own_here, load.at[0]), pltpu.make_async_copy(snd.at[0], snd_here, load.at[1])]
    copies = [pltpu.make_async_copy(own, out.at[0], load.at[2])]
    for copy in loads + copies:
        copy.start()
    for copy in loads:
        copy.wait()
    pl.semaphore_wait(barrier, 8)
    for n in range(8):
        copy = pltpu.make_async_remote_copy(
            src_ref=own_here, dst_ref=out.at[n + 1], send_sem=send.at[n], recv_sem=recv.at[n],
            device_id=around[n], device_id_type=MESH)
        copy.start()
        copies.append(copy)
    fields = extra_fields(snd_here[...], own_here[...])
    for a in range(16):
        columns(rest.at[a], jnp.concatenate([field[a:a + 1] for field in fields], 0), (0, 1, 2))
        copy = pltpu.make_async_copy(rest.at[a], rest_out.at[a], leave.at[a])
        copy.start()
        copies.append(copy)
    for copy in copies:
        copy.wait()


def share(own, snd):
    return pl.pallas_call(
        share_kernel,
        out_shape=(jax.ShapeDtypeStruct((9, 16, 256), jnp.float32), jax.ShapeDtypeStruct((16, 3, 256, 128), jnp.float32)),
        in_specs=[HBM] * 2, out_specs=(HBM,) * 2,
        scratch_shapes=[
            pltpu.VMEM((16, 256), jnp.float32),
            pltpu.VMEM((16, 256), jnp.float32),
            pltpu.VMEM((16, 3, 256, 128), jnp.float32),
            pltpu.SemaphoreType.DMA((3,)),
            pltpu.SemaphoreType.DMA((16,)),
            pltpu.SemaphoreType.DMA((8,)),
            pltpu.SemaphoreType.DMA((8,)),
        ],
        compiler_params=pltpu.CompilerParams(collective_id=1, has_side_effects=True, vmem_limit_bytes=WHOLE),
        name="share",
    )(own, snd)


def body(positions, velocities, masses, smoothing, sound2, counts, move_to, proxy_send, pairs):
    rec, snd, meta, cols = exchange(positions, velocities, masses, smoothing, sound2, counts, move_to, proxy_send.reshape(1, 128))
    rec = rec.reshape(144, 8, 256)
    rho, safe, tab, buf = density(rec, meta, pairs.T, cols)
    rho_all, rest = share(safe, snd)
    accel = force(rec, snd, rho_all, meta, tab, buf, cols, rest)
    return rho, accel


def solution(mesh):
    flat, cells, three = P(("gx", "gy")), P(("gx", "gy"), None), P(None, ("gx", "gy"), None)
    return jax.shard_map(
        body, mesh=mesh,
        in_specs=(three, three, cells, cells, cells, flat, flat, flat, cells),
        out_specs=(cells, three), check_vma=False)
```

```python
import math, functools
import jax, jax.numpy as jnp
from jax import lax
from jax.experimental import pallas as pl
from jax.experimental.pallas import tpu as pltpu

CELLS=16; SLOTS=256; NPAIRS=160; NORM=21.0/(16.0*math.pi)
WHOLE=63<<20
MAXT=2*NPAIRS+3*CELLS+8
PLACE=NPAIRS; FIRST=2*NPAIRS; LAST=FIRST+CELLS

def rcp(x):
    return pl.reciprocal(x, approx=True)

def append(buf, x0, x1, pos, lane):
    tile=lax.shift_right_logical(pos,7); s=lax.bitwise_and(pos,127)
    t0=pltpu.roll(x0,s,1); t1=pltpu.roll(x1,s,1)
    keep=lane>=s
    pltpu.store(buf.at[tile],t0,mask=keep)
    buf[tile+1]=jnp.where(keep,t1,t0)
    buf[tile+2]=jnp.where(keep,0.0,t1)

def plan(meta, pairs, tab, filled, count_of, place_of):
    for a in range(CELLS):
        filled[a]=0
    def size(p,_):
        a=pairs[0,p]; b=pairs[1,p]
        n=lax.shift_right_logical(b,4); r=lax.bitwise_and(b,15)
        cell=jnp.where(n==0,r,meta[n,1,jnp.maximum(n-1,0)*16+r])
        count=meta[n,0,cell]
        tab[p]=n*16+cell
        place_of[p]=n*16+meta[n,2,cell]
        count_of[p]=count
        filled[a]=filled[a]+count
        return 0
    lax.fori_loop(0,NPAIRS,size,0,unroll=8)
    tile=jnp.int32(0)
    for a in range(CELLS):
        end=tile+lax.shift_right_logical(filled[a]+127,7)
        tab[FIRST+a]=tile; tab[LAST+a]=end
        filled[a]=tile*128
        tile=end+2

def pack_main(rec, pairs, tab, filled, count_of, place_of, shifts, buf, unroll):
    lane=lax.broadcasted_iota(jnp.int32,(8,128),1)
    row=lax.broadcasted_iota(jnp.int32,(8,128),0)
    for d in range(27):
        dx,dy,dz=d//9-1,d//3%3-1,d%3-1
        shifts[d]=jnp.where(row==0,float(dx),jnp.where(row==1,float(dy),jnp.where(row==2,float(dz),0.0)))
    def put(p,_):
        a=pairs[0,p]
        pos=filled[a]
        filled[a]=pos+count_of[p]
        tab[PLACE+p]=pos
        src=place_of[p]; shift=shifts[pairs[2,p]]
        append(buf,rec[src,:,0:128]+shift,rec[src,:,128:256]+shift,pos,lane)
        return 0
    lax.fori_loop(0,NPAIRS,put,0,unroll=unroll)

def columns(icol, block, rows):
    for f,row in enumerate(rows):
        for half in range(2):
            lanes=slice(128*half,128*half+128)
            icol[f,lanes,:]=jnp.broadcast_to(block[row:row+1,lanes],(128,128)).T

def extra_fields(c2, rho):
    return 0.5*(c2*lax.rsqrt(c2)),c2*rcp(rho),rho

def fetch(pairs_of_refs, sems):
    copies=[pltpu.make_async_copy(src,dst,sems.at[k]) for k,(src,dst) in enumerate(pairs_of_refs)]
    for copy in copies:
        copy.start()
    return copies

def density_kernel(J64,JREST,U,rec_in,meta_in,pairs_in,cols_in,rho,safe,tab,buf_out,rec,meta,pairs,buf,sems,filled,count_of,place_of,shifts,cols,col_sems,acc):
    copies=fetch(((meta_in,meta),(pairs_in,pairs),(rec_in,rec)),sems)
    copies[0].wait(); copies[1].wait()
    def column_copy(a):
        return pltpu.make_async_copy(cols_in.at[meta[0,2,a],pl.ds(0,4)],cols.at[a],col_sems.at[a])
    def ask(a,_):
        column_copy(a).start()
        return 0
    lax.fori_loop(0,CELLS,ask,0)
    plan(meta,pairs,tab,filled,count_of,place_of)
    copies[2].wait()
    pack_main(rec,pairs,tab,filled,count_of,place_of,shifts,buf,U)
    leave=pltpu.make_async_copy(buf,buf_out,sems.at[3])
    leave.start()
    def cell(a,_):
        column_copy(a).wait()
        icol=cols.at[a]
        first=tab[FIRST+a]; last=tab[LAST+a]
        count=meta[0,0,a]
        def iblock(IB,JB,start,_):
            rows=pl.ds(pl.multiple_of(start,8),IB)
            nfull=(last-first)//JB
            xi,yi,zi,hi=(icol[f,rows,:] for f in range(4))
            def tile(t):
                j=lambda rw: buf[t,rw:rw+1,:]
                dx=xi-j(0); dy=yi-j(1); dz=zi-j(2)
                r2=dx*dx+dy*dy+dz*dz
                s=hi+j(4)
                u=rcp(s*lax.rsqrt(r2))
                t_=jnp.maximum(1.0-u,0.0)
                w=t_*rcp(s)
                return (w*w)*(w*t_)*((1.25-t_)*j(3))
            def many(k,total):
                t=first+k*JB
                return total+functools.reduce(lambda p,q:p+q,[tile(t+i) for i in range(JB)])
            total=lax.fori_loop(0,nfull,many,jnp.zeros((IB,128),jnp.float32))
            if JB>1:
                total=lax.fori_loop(first+nfull*JB,last,lambda t,tt:tt+tile(t),total)
            acc[a,rows,:]=total
            return 0
        groups=lax.shift_right_logical(count+7,3)
        rest=lax.bitwise_and(groups,7)
        big=lax.shift_right_logical(groups,3)-jnp.where(rest==1,1,0)
        lax.fori_loop(0,big,lambda g,c:iblock(64,J64,g*64,c),0)
        for r,n in enumerate(JREST,1):
            lax.fori_loop(0,jnp.where(rest==r,1,0),lambda g,c:iblock(72 if r==1 else 8*r,n,big*64,c),0)
        return 0
    lax.fori_loop(0,CELLS,cell,0)
    for a in range(CELLS):
        sums=jnp.sum(acc[a].T,axis=0,keepdims=True)
        there=rec[meta[0,2,a],3:4,:]>0
        rho[a:a+1,:]=jnp.where(there,(32.0*NORM)*sums,0.0)
        safe[a:a+1,:]=jnp.where(there,(32.0*NORM)*sums,1.0)
    leave.wait()

def density(rec,meta,pairs,cols,J64=2,JREST=(2,4,4,4,3,2,2),U=8):
    V=pl.BlockSpec(memory_space=pltpu.VMEM); S=pl.BlockSpec(memory_space=pltpu.SMEM); H=pl.BlockSpec(memory_space=pltpu.HBM)
    return pl.pallas_call(functools.partial(density_kernel,J64,JREST,U),
        out_shape=(jax.ShapeDtypeStruct((CELLS,SLOTS),jnp.float32),jax.ShapeDtypeStruct((CELLS,SLOTS),jnp.float32),jax.ShapeDtypeStruct((384,),jnp.int32),jax.ShapeDtypeStruct((MAXT,8,128),jnp.float32)),
        in_specs=[H,H,H,H],out_specs=(V,V,S,H),
        scratch_shapes=[pltpu.VMEM((144,8,SLOTS),jnp.float32),pltpu.SMEM((9,4,128),jnp.int32),pltpu.SMEM((3,NPAIRS),jnp.int32),pltpu.VMEM((MAXT,8,128),jnp.float32),pltpu.SemaphoreType.DMA((4,)),pltpu.SMEM((CELLS,),jnp.int32),pltpu.SMEM((NPAIRS,),jnp.int32),pltpu.SMEM((NPAIRS,),jnp.int32),pltpu.VMEM((27,8,128),jnp.float32),pltpu.VMEM((CELLS,4,SLOTS,128),jnp.float32),pltpu.SemaphoreType.DMA((CELLS,)),pltpu.VMEM((CELLS,SLOTS,128),jnp.float32)],
        compiler_params=pltpu.CompilerParams(vmem_limit_bytes=WHOLE),
        name="density")(rec,meta,pairs,cols)

def force_kernel(J32,JREST,U,rec_in,snd_in,rho_in,meta_in,tab_in,buf_in,cols_in,rest_in,out,rec,snd,rho,meta,tab,buf,sems,extra,cells,cols,col_sems,acc):
    copies=fetch(((snd_in,snd),(rho_in,rho),(tab_in,tab),(meta_in.at[0],meta.at[0]),(rec_in.at[pl.ds(0,CELLS)],rec),(buf_in,buf)),sems)
    copies[3].wait()
    def column_copy(a):
        return (pltpu.make_async_copy(cols_in.at[meta[0,2,a]],cols.at[a,pl.ds(0,7)],col_sems.at[0,a]),
                pltpu.make_async_copy(rest_in.at[a],cols.at[a,pl.ds(7,3)],col_sems.at[1,a]))
    def ask(a,_):
        for copy in column_copy(a):
            copy.start()
        return 0
    lax.fori_loop(0,CELLS,ask,0)
    for copy in copies[:3]:
        copy.wait()
    for n in range(9):
        for half in range(2):
            c8=slice(8*half,8*half+8)
            c2=snd[n,c8,:]; rr=rho[n,c8,:]
            base=(n*16+8*half)*8
            for f,val in enumerate(extra_fields(c2,rr)):
                cells[0,pl.ds(base+f,8,stride=8),:]=val[:,0:128]
                cells[1,pl.ds(base+f,8,stride=8),:]=val[:,128:256]
    lane=lax.broadcasted_iota(jnp.int32,(8,128),1)
    block=lambda src: pl.ds(pl.multiple_of(src*8,8),8)
    def put(p,_):
        src=tab[p]
        append(extra,cells[0,block(src),:],cells[1,block(src),:],tab[PLACE+p],lane)
        return 0
    lax.fori_loop(0,NPAIRS,put,0,unroll=U)
    for copy in copies[4:]:
        copy.wait()
    def cell(a,_):
        for copy in column_copy(a):
            copy.wait()
        first=tab[FIRST+a]; last=tab[LAST+a]
        count=meta[0,0,a]
        def iblock(IB,JB,start,_):
            rows=pl.ds(pl.multiple_of(start,8),IB)
            nfull=(last-first)//JB
            def tile(t):
                i=lambda f: cols[a,f,rows,:]
                j=lambda rw: buf[t,rw:rw+1,:]
                e=lambda rw: extra[t,rw:rw+1,:]
                dx=i(0)-j(0); dy=i(1)-j(1); dz=i(2)-j(2)
                r2=dx*dx+dy*dy+dz*dz
                s=i(3)+j(4)
                inv=rcp(s)
                u=rcp(s*lax.rsqrt(r2))
                w=jnp.maximum(1.0-u,0.0)*inv
                va=jnp.minimum((i(4)-j(5))*dx+(i(5)-j(6))*dy+(i(6)-j(7))*dz,0.0)
                m=va*inv*rcp(u*u+0.0025)
                visc=m*((m-i(7))-e(0))*rcp(i(9)+e(2))
                f=(i(8)+e(1)+visc)*j(3)*((w*w)*(w*(inv*inv)))
                return f*dx,f*dy,f*dz
            def many(k,total):
                t=first+k*JB
                ts=[tile(t+q) for q in range(JB)]
                return tuple(total[c]+functools.reduce(lambda p,q:p+q,[x[c] for x in ts]) for c in range(3))
            z=jnp.zeros((IB,128),jnp.float32)
            total=lax.fori_loop(0,nfull,many,(z,z,z))
            if JB>1:
                def one(t,tt):
                    x=tile(t)
                    return tuple(p+q for p,q in zip(tt,x))
                total=lax.fori_loop(first+nfull*JB,last,one,total)
            for c in range(3):
                acc[c,a,rows,:]=total[c]
            return 0
        groups=lax.shift_right_logical(count+7,3)
        rest=lax.bitwise_and(groups,3)
        big=lax.shift_right_logical(groups,2)-jnp.where(rest==1,1,0)
        lax.fori_loop(0,big,lambda g,c:iblock(32,J32,g*32,c),0)
        for r,n in enumerate(JREST,1):
            lax.fori_loop(0,jnp.where(rest==r,1,0),lambda g,c:iblock(40 if r==1 else 8*r,n,big*32,c),0)
        return 0
    lax.fori_loop(0,CELLS,cell,0)
    for a in range(CELLS):
        for c in range(3):
            sums=jnp.sum(acc[c,a].T,axis=0,keepdims=True)
            out[c,a:a+1,:]=jnp.where(rec[meta[0,2,a],3:4,:]>0,(160.0*NORM)*sums,0.0)

def force(rec,snd,rho,meta,tab,buf,cols,rest,J32=4,JREST=(4,4,4),U=16):
    V=pl.BlockSpec(memory_space=pltpu.VMEM); S=pl.BlockSpec(memory_space=pltpu.SMEM); H=pl.BlockSpec(memory_space=pltpu.HBM)
    return pl.pallas_call(functools.partial(force_kernel,J32,JREST,U),
        out_shape=jax.ShapeDtypeStruct((3,CELLS,SLOTS),jnp.float32),
        in_specs=[H]*8,out_specs=V,
        scratch_shapes=[pltpu.VMEM((CELLS,8,SLOTS),jnp.float32),pltpu.VMEM((9,CELLS,SLOTS),jnp.float32),pltpu.VMEM((9,CELLS,SLOTS),jnp.float32),pltpu.SMEM((1,4,128),jnp.int32),pltpu.SMEM((384,),jnp.int32),pltpu.VMEM((MAXT,8,128),jnp.float32),pltpu.SemaphoreType.DMA((6,)),pltpu.VMEM((MAXT,8,128),jnp.float32),pltpu.VMEM((2,144*8,128),jnp.float32),pltpu.VMEM((CELLS,10,SLOTS,128),jnp.float32),pltpu.SemaphoreType.DMA((2,CELLS)),pltpu.VMEM((3,CELLS,SLOTS,128),jnp.float32)],
        compiler_params=pltpu.CompilerParams(vmem_limit_bytes=WHOLE),
        name="force")(rec,snd,rho,meta,tab,buf,cols,rest)


from jax.sharding import PartitionSpec as P

N_GX=16; N_GY=8
AROUND=((-1,-1),(-1,0),(-1,1),(0,-1),(0,1),(1,-1),(1,0),(1,1))
MESH=pl.DeviceIdType.MESH
FAR_FIRST=(6, 10, 7, 9, 2, 14, 5, 11, 8, 3, 13, 1, 15, 4, 12)
OWN_FIELDS=(0, 1, 2, 4, 5, 6, 7)


def neighbours(u, w):
    return [(lax.rem(u + du + N_GX, N_GX), lax.rem(w + dw + N_GY, N_GY)) for du, dw in AROUND]


def exchange_kernel(*refs):
    given, (rec_out, snd_out, meta_out, cols_out), scratch = refs[:8], refs[8:12], refs[12:]
    held, (rec, outbox, inbox, outbox2, inbox2, metas, moved, sounds_moved, cols, load, leave, send1, recv1, send2, recv2) = scratch[:8], scratch[8:]
    pos, vel, mass, smooth, snd, counts, move, lists = held
    u, w = lax.axis_index("gx"), lax.axis_index("gy")
    loads = [pltpu.make_async_copy(src, dst, load.at[k]) for k, (src, dst) in enumerate(zip(given, held))]
    for copy in loads:
        copy.start()
    around = neighbours(u, w)
    barrier = pltpu.get_barrier_semaphore()
    for off in range(1, N_GX):
        pl.semaphore_signal(barrier, inc=1, device_id=(lax.rem(u + off, N_GX), w), device_id_type=MESH)
    for n in (3, 4):
        pl.semaphore_signal(barrier, inc=1, device_id=around[n], device_id_type=MESH)

    for copy in loads:
        copy.wait()
    slot = lax.broadcasted_iota(jnp.int32, (1, 256), 1)
    for c in range(16):
        for f in range(3):
            rec[c, f:f + 1, :] = pos[f, c:c + 1, :]
            rec[c, 5 + f:6 + f, :] = vel[f, c:c + 1, :]
        rec[c, 3:4, :] = jnp.where(slot < counts[c], mass[c:c + 1, :], 0.0)
        rec[c, 4:5, :] = smooth[c:c + 1, :]

    headed = [lax.shift_right_logical(move[c], 7) for c in range(16)]
    row = lax.broadcasted_iota(jnp.int32, (8, 256), 0)

    def post(off, _):
        column = lax.rem(u + off, N_GX)
        first, last = jnp.int32(16), jnp.int32(-1)
        for c in range(16):
            match = headed[c] == column
            first = jnp.minimum(first, jnp.where(match, c, 16))
            last = jnp.where(match, c, last)
        found = last >= 0
        first = jnp.where(found, first, 0)
        last = jnp.where(found, last, 0)
        outbox[off, 0:8, :] = rec[first]
        outbox2[off] = rec[last]
        number = lambda c: jnp.where(found, move[c], -1).astype(jnp.float32)
        amount = lambda c: counts[c].astype(jnp.float32)
        more = jnp.where(row == 0, snd[pl.ds(first, 1), :], snd[pl.ds(last, 1), :])
        more = jnp.where(row == 2, number(first), more)
        more = jnp.where(row == 3, number(last), more)
        more = jnp.where(row == 4, amount(first), more)
        more = jnp.where(row == 5, amount(last), more)
        outbox[off, 8:16, :] = more
        return 0

    lax.fori_loop(0, N_GX, post, 0)
    pl.semaphore_wait(barrier, N_GX - 1 + 2)

    def parcel(off, part):
        src, dst = ((outbox, inbox), (outbox2, inbox2))[part]
        return pltpu.make_async_remote_copy(
            src_ref=src.at[off], dst_ref=dst.at[off], send_sem=send1.at[part, off], recv_sem=recv1.at[part, off],
            device_id=(lax.rem(u + off, N_GX), w), device_id_type=MESH)

    for part in range(2):
        for off in FAR_FIRST:
            parcel(off, part).start()
    inbox[0] = outbox[0]
    inbox2[0] = outbox2[0]

    first_own = ((u * N_GY + w) * 16).astype(jnp.float32)
    sub = lax.broadcasted_iota(jnp.int32, (16, 256), 0).astype(jnp.float32) + first_own
    lane = lax.broadcasted_iota(jnp.int32, (1, 128), 1).astype(jnp.float32) + first_own

    def place(cells, block, number, rank):
        key = jnp.broadcast_to(jnp.where(number >= 0.0, rank, -1.0), (8, 256))
        cells = tuple(jnp.where(key == float(k), block, cells[k]) for k in range(8))
        return cells, rank + jnp.where(number >= 0.0, 1.0, 0.0)

    def absorb(off, carry):
        cells, rank, sounds, amounts, ranks = carry
        for k in range(2):
            number = inbox[off, 10 + k:11 + k, :]
            mine = lane == number[:, 0:128]
            sounds = jnp.where(sub == number, inbox[off, 8 + k:9 + k, :], sounds)
            amounts = jnp.where(mine, inbox[off, 12 + k:13 + k, 0:128], amounts)
            ranks = jnp.where(mine, rank[:, 0:128] + 8.0 * k, ranks)
        cells, rank = place(cells, inbox[off, 0:8, :], inbox[off, 10:11, :], rank)
        return cells, rank, sounds, amounts, ranks

    def absorb_next(off, carry):
        parcel(off, 0).wait_recv()
        return absorb(off, carry)

    def absorb2(off, carry):
        return place(carry[0], inbox2[off], inbox[off, 10:11, :], carry[1])

    def absorb2_next(off, carry):
        parcel(off, 1).wait_recv()
        return absorb2(off, carry)

    zero = jnp.zeros((8, 256), jnp.float32)
    line = jnp.zeros((1, 128), jnp.float32)
    none = ((zero,) * 8, jnp.zeros((1, 256), jnp.float32))
    carry = absorb(0, none + (jnp.zeros((16, 256), jnp.float32), line, line))
    cells, _, sounds, amounts, ranks = lax.fori_loop(1, N_GX, absorb_next, carry)
    for k in range(8):
        moved[k] = cells[k]
    sounds_moved[...] = sounds
    metas[0:1, :] = amounts.astype(jnp.int32)
    metas[1:2, :] = lists[...]
    metas[2:3, :] = ranks.astype(jnp.int32)
    metas[3:4, :] = lists[...]

    halves = (pl.ds(0, 8), pl.ds(8, 8))
    own = (metas, moved.at[halves[0]], sounds_moved, moved.at[halves[1]])
    at = lambda n: (meta_out.at[n], rec_out.at[n, halves[0]], snd_out.at[n], rec_out.at[n, halves[1]])
    remote = lambda src, n, k, device: pltpu.make_async_remote_copy(
        src_ref=src, dst_ref=at(n + 1)[k], send_sem=send2.at[n, k], recv_sem=recv2.at[n, k],
        device_id=device, device_id_type=MESH)
    copies, arriving = [], {}

    def spread_out(items):
        for nearest in ((1, 6), (3, 4)):
            for k in items:
                for n in nearest:
                    copy = remote(own[k], n, k, around[n])
                    copy.start()
                    if nearest == (1, 6):
                        arriving[n, k] = copy
                    else:
                        copies.append(copy)

    def pass_on(items):
        for k in items:
            for n in (1, 6):
                arriving[n, k].wait_recv()
                for to, step in ((n - 1, 3), (n + 1, 4)):
                    copy = remote(at(n + 1)[k], to, k, around[step])
                    copy.start()
                    copies.append(copy)

    def column_copy(k):
        return pltpu.make_async_copy(cols.at[k], cols_out.at[k], leave.at[k])

    def make_columns(k, _):
        columns(cols.at[k], moved[k], OWN_FIELDS)
        column_copy(k).start()
        return 0

    spread_out((0, 1, 2))
    cells, _ = lax.fori_loop(1, N_GX, absorb2_next, absorb2(0, none))
    for k in range(8):
        moved[8 + k] = cells[k]
    spread_out((3,))
    for k in range(4):
        copy = pltpu.make_async_copy(own[k], at(0)[k], load.at[k])
        copy.start()
        copies.append(copy)
    pass_on((0, 1, 2, 3))
    lax.fori_loop(0, 16, make_columns, 0)
    for copy in arriving.values():
        copy.wait_send()

    def left(k, _):
        column_copy(k).wait()
        return 0

    lax.fori_loop(0, 16, left, 0)

    def sent(off, _):
        parcel(off, 0).wait_send()
        parcel(off, 1).wait_send()
        return 0

    lax.fori_loop(1, N_GX, sent, 0)
    for copy in copies:
        copy.wait()


VMEM=pl.BlockSpec(memory_space=pltpu.VMEM)
HBM=pl.BlockSpec(memory_space=pltpu.HBM)

def exchange(positions, velocities, masses, smoothing, sound2, counts, move_to, lists):
    return pl.pallas_call(
        exchange_kernel,
        out_shape=(jax.ShapeDtypeStruct((9, 16, 8, 256), jnp.float32),
                   jax.ShapeDtypeStruct((9, 16, 256), jnp.float32),
                   jax.ShapeDtypeStruct((9, 4, 128), jnp.int32),
                   jax.ShapeDtypeStruct((16, 7, 256, 128), jnp.float32)),
        in_specs=[HBM] * 8,
        out_specs=(HBM,) * 4,
        scratch_shapes=[
            pltpu.VMEM((3, 16, 256), jnp.float32),
            pltpu.VMEM((3, 16, 256), jnp.float32),
            pltpu.VMEM((16, 256), jnp.float32),
            pltpu.VMEM((16, 256), jnp.float32),
            pltpu.VMEM((16, 256), jnp.float32),
            pltpu.SMEM((16,), jnp.int32),
            pltpu.SMEM((16,), jnp.int32),
            pltpu.VMEM((1, 128), jnp.int32),
            pltpu.VMEM((16, 8, 256), jnp.float32),
            pltpu.VMEM((N_GX, 16, 256), jnp.float32),
            pltpu.VMEM((N_GX, 16, 256), jnp.float32),
            pltpu.VMEM((N_GX, 8, 256), jnp.float32),
            pltpu.VMEM((N_GX, 8, 256), jnp.float32),
            pltpu.VMEM((4, 128), jnp.int32),
            pltpu.VMEM((16, 8, 256), jnp.float32),
            pltpu.VMEM((16, 256), jnp.float32),
            pltpu.VMEM((16, 7, 256, 128), jnp.float32),
            pltpu.SemaphoreType.DMA((8,)),
            pltpu.SemaphoreType.DMA((16,)),
            pltpu.SemaphoreType.DMA((2, N_GX)),
            pltpu.SemaphoreType.DMA((2, N_GX)),
            pltpu.SemaphoreType.DMA((8, 4)),
            pltpu.SemaphoreType.DMA((8, 4)),
        ],
        compiler_params=pltpu.CompilerParams(collective_id=0, has_side_effects=True, vmem_limit_bytes=WHOLE),
        name="exchange",
    )(positions, velocities, masses, smoothing, sound2, counts, move_to, lists)


def share_kernel(own, snd, out, rest_out, own_here, snd_here, rest, load, leave, send, recv):
    u, w = lax.axis_index("gx"), lax.axis_index("gy")
    around = neighbours(u, w)
    barrier = pltpu.get_barrier_semaphore()
    for n in range(8):
        pl.semaphore_signal(barrier, inc=1, device_id=around[n], device_id_type=MESH)
    loads = [pltpu.make_async_copy(own, own_here, load.at[0]), pltpu.make_async_copy(snd.at[0], snd_here, load.at[1])]
    copies = [pltpu.make_async_copy(own, out.at[0], load.at[2])]
    for copy in loads + copies:
        copy.start()
    for copy in loads:
        copy.wait()
    pl.semaphore_wait(barrier, 8)
    for n in range(8):
        copy = pltpu.make_async_remote_copy(
            src_ref=own_here, dst_ref=out.at[n + 1], send_sem=send.at[n], recv_sem=recv.at[n],
            device_id=around[n], device_id_type=MESH)
        copy.start()
        copies.append(copy)
    fields = extra_fields(snd_here[...], own_here[...])
    for a in range(16):
        columns(rest.at[a], jnp.concatenate([field[a:a + 1] for field in fields], 0), (0, 1, 2))
        copy = pltpu.make_async_copy(rest.at[a], rest_out.at[a], leave.at[a])
        copy.start()
        copies.append(copy)
    for copy in copies:
        copy.wait()


def share(own, snd):
    return pl.pallas_call(
        share_kernel,
        out_shape=(jax.ShapeDtypeStruct((9, 16, 256), jnp.float32), jax.ShapeDtypeStruct((16, 3, 256, 128), jnp.float32)),
        in_specs=[HBM] * 2, out_specs=(HBM,) * 2,
        scratch_shapes=[
            pltpu.VMEM((16, 256), jnp.float32),
            pltpu.VMEM((16, 256), jnp.float32),
            pltpu.VMEM((16, 3, 256, 128), jnp.float32),
            pltpu.SemaphoreType.DMA((3,)),
            pltpu.SemaphoreType.DMA((16,)),
            pltpu.SemaphoreType.DMA((8,)),
            pltpu.SemaphoreType.DMA((8,)),
        ],
        compiler_params=pltpu.CompilerParams(collective_id=1, has_side_effects=True, vmem_limit_bytes=WHOLE),
        name="share",
    )(own, snd)


def body(positions, velocities, masses, smoothing, sound2, counts, move_to, proxy_send, pairs):
    rec, snd, meta, cols = exchange(positions, velocities, masses, smoothing, sound2, counts, move_to, proxy_send.reshape(1, 128))
    rec = rec.reshape(144, 8, 256)
    rho, safe, tab, buf = density(rec, meta, pairs.T, cols)
    rho_all, rest = share(safe, snd)
    accel = force(rec, snd, rho_all, meta, tab, buf, cols, rest)
    return rho, accel


def solution(mesh):
    flat, cells, three = P(("gx", "gy")), P(("gx", "gy"), None), P(None, ("gx", "gy"), None)
    return jax.shard_map(
        body, mesh=mesh,
        in_specs=(three, three, cells, cells, cells, flat, flat, flat, cells),
        out_specs=(cells, three), check_vma=False)
```

```python
import math, functools
import jax, jax.numpy as jnp
from jax import lax
from jax.experimental import pallas as pl
from jax.experimental.pallas import tpu as pltpu

CELLS=16; SLOTS=256; NPAIRS=160; NORM=21.0/(16.0*math.pi)
WHOLE=63<<20
MAXT=2*NPAIRS+3*CELLS+8
PLACE=NPAIRS; FIRST=2*NPAIRS; LAST=FIRST+CELLS

def rcp(x):
    return pl.reciprocal(x, approx=True)

def append(buf, x0, x1, pos, lane):
    tile=lax.shift_right_logical(pos,7); s=lax.bitwise_and(pos,127)
    t0=pltpu.roll(x0,s,1); t1=pltpu.roll(x1,s,1)
    keep=lane>=s
    pltpu.store(buf.at[tile],t0,mask=keep)
    buf[tile+1]=jnp.where(keep,t1,t0)
    buf[tile+2]=jnp.where(keep,0.0,t1)

def plan(meta, pairs, tab, filled, count_of, place_of):
    for a in range(CELLS):
        filled[a]=0
    def size(p,_):
        a=pairs[0,p]; b=pairs[1,p]
        n=lax.shift_right_logical(b,4); r=lax.bitwise_and(b,15)
        cell=jnp.where(n==0,r,meta[n,1,jnp.maximum(n-1,0)*16+r])
        count=meta[n,0,cell]
        tab[p]=n*16+cell
        place_of[p]=n*16+meta[n,2,cell]
        count_of[p]=count
        filled[a]=filled[a]+count
        return 0
    lax.fori_loop(0,NPAIRS,size,0,unroll=8)
    tile=jnp.int32(0)
    for a in range(CELLS):
        end=tile+lax.shift_right_logical(filled[a]+127,7)
        tab[FIRST+a]=tile; tab[LAST+a]=end
        filled[a]=tile*128
        tile=end+2

def pack_main(rec, pairs, tab, filled, count_of, place_of, shifts, buf, unroll):
    lane=lax.broadcasted_iota(jnp.int32,(8,128),1)
    row=lax.broadcasted_iota(jnp.int32,(8,128),0)
    for d in range(27):
        dx,dy,dz=d//9-1,d//3%3-1,d%3-1
        shifts[d]=jnp.where(row==0,float(dx),jnp.where(row==1,float(dy),jnp.where(row==2,float(dz),0.0)))
    def put(p,_):
        a=pairs[0,p]
        pos=filled[a]
        filled[a]=pos+count_of[p]
        tab[PLACE+p]=pos
        src=place_of[p]; shift=shifts[pairs[2,p]]
        append(buf,rec[src,:,0:128]+shift,rec[src,:,128:256]+shift,pos,lane)
        return 0
    lax.fori_loop(0,NPAIRS,put,0,unroll=unroll)

def columns(icol, block, rows):
    for f,row in enumerate(rows):
        for half in range(2):
            lanes=slice(128*half,128*half+128)
            icol[f,lanes,:]=jnp.broadcast_to(block[row:row+1,lanes],(128,128)).T

def extra_fields(c2, rho):
    return 0.5*(c2*lax.rsqrt(c2)),c2*rcp(rho),rho

def fetch(pairs_of_refs, sems):
    copies=[pltpu.make_async_copy(src,dst,sems.at[k]) for k,(src,dst) in enumerate(pairs_of_refs)]
    for copy in copies:
        copy.start()
    return copies

def density_kernel(J64,JREST,U,rec_in,meta_in,pairs_in,cols_in,rho,safe,tab,buf_out,rec,meta,pairs,buf,sems,filled,count_of,place_of,shifts,cols,col_sems,acc):
    copies=fetch(((meta_in,meta),(pairs_in,pairs),(rec_in,rec)),sems)
    copies[0].wait(); copies[1].wait()
    def column_copy(a):
        return pltpu.make_async_copy(cols_in.at[meta[0,2,a],pl.ds(0,4)],cols.at[a],col_sems.at[a])
    def ask(a,_):
        column_copy(a).start()
        return 0
    lax.fori_loop(0,CELLS,ask,0)
    plan(meta,pairs,tab,filled,count_of,place_of)
    copies[2].wait()
    pack_main(rec,pairs,tab,filled,count_of,place_of,shifts,buf,U)
    leave=pltpu.make_async_copy(buf,buf_out,sems.at[3])
    leave.start()
    def cell(a,_):
        column_copy(a).wait()
        icol=cols.at[a]
        first=tab[FIRST+a]; last=tab[LAST+a]
        count=meta[0,0,a]
        def iblock(IB,JB,start,_):
            rows=pl.ds(pl.multiple_of(start,8),IB)
            nfull=(last-first)//JB
            xi,yi,zi,hi=(icol[f,rows,:] for f in range(4))
            def tile(t):
                j=lambda rw: buf[t,rw:rw+1,:]
                dx=xi-j(0); dy=yi-j(1); dz=zi-j(2)
                r2=dx*dx+dy*dy+dz*dz
                s=hi+j(4)
                u=rcp(s*lax.rsqrt(r2))
                t_=jnp.maximum(1.0-u,0.0)
                w=t_*rcp(s)
                return (w*w)*(w*t_)*((1.25-t_)*j(3))
            def many(k,total):
                t=first+k*JB
                return total+functools.reduce(lambda p,q:p+q,[tile(t+i) for i in range(JB)])
            total=lax.fori_loop(0,nfull,many,jnp.zeros((IB,128),jnp.float32))
            if JB>1:
                total=lax.fori_loop(first+nfull*JB,last,lambda t,tt:tt+tile(t),total)
            acc[a,rows,:]=total
            return 0
        groups=lax.shift_right_logical(count+7,3)
        rest=lax.bitwise_and(groups,7)
        big=lax.shift_right_logical(groups,3)-jnp.where(rest==1,1,0)
        lax.fori_loop(0,big,lambda g,c:iblock(64,J64,g*64,c),0)
        for r,n in enumerate(JREST,1):
            lax.fori_loop(0,jnp.where(rest==r,1,0),lambda g,c:iblock(72 if r==1 else 8*r,n,big*64,c),0)
        return 0
    lax.fori_loop(0,CELLS,cell,0)
    for a in range(CELLS):
        sums=jnp.sum(acc[a].T,axis=0,keepdims=True)
        there=rec[meta[0,2,a],3:4,:]>0
        rho[a:a+1,:]=jnp.where(there,(32.0*NORM)*sums,0.0)
        safe[a:a+1,:]=jnp.where(there,(32.0*NORM)*sums,1.0)
    leave.wait()

def density(rec,meta,pairs,cols,J64=2,JREST=(2,4,4,4,3,2,2),U=16):
    V=pl.BlockSpec(memory_space=pltpu.VMEM); S=pl.BlockSpec(memory_space=pltpu.SMEM); H=pl.BlockSpec(memory_space=pltpu.HBM)
    return pl.pallas_call(functools.partial(density_kernel,J64,JREST,U),
        out_shape=(jax.ShapeDtypeStruct((CELLS,SLOTS),jnp.float32),jax.ShapeDtypeStruct((CELLS,SLOTS),jnp.float32),jax.ShapeDtypeStruct((384,),jnp.int32),jax.ShapeDtypeStruct((MAXT,8,128),jnp.float32)),
        in_specs=[H,H,H,H],out_specs=(V,V,S,H),
        scratch_shapes=[pltpu.VMEM((144,8,SLOTS),jnp.float32),pltpu.SMEM((9,4,128),jnp.int32),pltpu.SMEM((3,NPAIRS),jnp.int32),pltpu.VMEM((MAXT,8,128),jnp.float32),pltpu.SemaphoreType.DMA((4,)),pltpu.SMEM((CELLS,),jnp.int32),pltpu.SMEM((NPAIRS,),jnp.int32),pltpu.SMEM((NPAIRS,),jnp.int32),pltpu.VMEM((27,8,128),jnp.float32),pltpu.VMEM((CELLS,4,SLOTS,128),jnp.float32),pltpu.SemaphoreType.DMA((CELLS,)),pltpu.VMEM((CELLS,SLOTS,128),jnp.float32)],
        compiler_params=pltpu.CompilerParams(vmem_limit_bytes=WHOLE),
        name="density")(rec,meta,pairs,cols)

def force_kernel(J32,JREST,U,rec_in,snd_in,rho_in,meta_in,tab_in,buf_in,cols_in,rest_in,out,rec,snd,rho,meta,tab,buf,sems,extra,cells,cols,col_sems,acc):
    copies=fetch(((snd_in,snd),(rho_in,rho),(tab_in,tab),(meta_in.at[0],meta.at[0]),(rec_in.at[pl.ds(0,CELLS)],rec),(buf_in,buf)),sems)
    copies[3].wait()
    def column_copy(a):
        return (pltpu.make_async_copy(cols_in.at[meta[0,2,a]],cols.at[a,pl.ds(0,7)],col_sems.at[0,a]),
                pltpu.make_async_copy(rest_in.at[a],cols.at[a,pl.ds(7,3)],col_sems.at[1,a]))
    def ask(a,_):
        for copy in column_copy(a):
            copy.start()
        return 0
    lax.fori_loop(0,CELLS,ask,0)
    for copy in copies[:3]:
        copy.wait()
    for n in range(9):
        for half in range(2):
            c8=slice(8*half,8*half+8)
            c2=snd[n,c8,:]; rr=rho[n,c8,:]
            base=(n*16+8*half)*8
            for f,val in enumerate(extra_fields(c2,rr)):
                cells[0,pl.ds(base+f,8,stride=8),:]=val[:,0:128]
                cells[1,pl.ds(base+f,8,stride=8),:]=val[:,128:256]
    lane=lax.broadcasted_iota(jnp.int32,(8,128),1)
    block=lambda src: pl.ds(pl.multiple_of(src*8,8),8)
    def put(p,_):
        src=tab[p]
        append(extra,cells[0,block(src),:],cells[1,block(src),:],tab[PLACE+p],lane)
        return 0
    lax.fori_loop(0,NPAIRS,put,0,unroll=U)
    for copy in copies[4:]:
        copy.wait()
    def cell(a,_):
        for copy in column_copy(a):
            copy.wait()
        first=tab[FIRST+a]; last=tab[LAST+a]
        count=meta[0,0,a]
        def iblock(IB,JB,start,_):
            rows=pl.ds(pl.multiple_of(start,8),IB)
            nfull=(last-first)//JB
            def tile(t):
                i=lambda f: cols[a,f,rows,:]
                j=lambda rw: buf[t,rw:rw+1,:]
                e=lambda rw: extra[t,rw:rw+1,:]
                dx=i(0)-j(0); dy=i(1)-j(1); dz=i(2)-j(2)
                r2=dx*dx+dy*dy+dz*dz
                s=i(3)+j(4)
                inv=rcp(s)
                u=rcp(s*lax.rsqrt(r2))
                w=jnp.maximum(1.0-u,0.0)*inv
                va=jnp.minimum((i(4)-j(5))*dx+(i(5)-j(6))*dy+(i(6)-j(7))*dz,0.0)
                m=va*inv*rcp(u*u+0.0025)
                visc=m*((m-i(7))-e(0))*rcp(i(9)+e(2))
                f=(i(8)+e(1)+visc)*j(3)*((w*w)*(w*(inv*inv)))
                return f*dx,f*dy,f*dz
            def many(k,total):
                t=first+k*JB
                ts=[tile(t+q) for q in range(JB)]
                return tuple(total[c]+functools.reduce(lambda p,q:p+q,[x[c] for x in ts]) for c in range(3))
            z=jnp.zeros((IB,128),jnp.float32)
            total=lax.fori_loop(0,nfull,many,(z,z,z))
            if JB>1:
                def one(t,tt):
                    x=tile(t)
                    return tuple(p+q for p,q in zip(tt,x))
                total=lax.fori_loop(first+nfull*JB,last,one,total)
            for c in range(3):
                acc[c,a,rows,:]=total[c]
            return 0
        groups=lax.shift_right_logical(count+7,3)
        rest=lax.bitwise_and(groups,3)
        big=lax.shift_right_logical(groups,2)-jnp.where(rest==1,1,0)
        lax.fori_loop(0,big,lambda g,c:iblock(32,J32,g*32,c),0)
        for r,n in enumerate(JREST,1):
            lax.fori_loop(0,jnp.where(rest==r,1,0),lambda g,c:iblock(40 if r==1 else 8*r,n,big*32,c),0)
        return 0
    lax.fori_loop(0,CELLS,cell,0)
    for a in range(CELLS):
        for c in range(3):
            sums=jnp.sum(acc[c,a].T,axis=0,keepdims=True)
            out[c,a:a+1,:]=jnp.where(rec[meta[0,2,a],3:4,:]>0,(160.0*NORM)*sums,0.0)

def force(rec,snd,rho,meta,tab,buf,cols,rest,J32=4,JREST=(4,4,4),U=16):
    V=pl.BlockSpec(memory_space=pltpu.VMEM); S=pl.BlockSpec(memory_space=pltpu.SMEM); H=pl.BlockSpec(memory_space=pltpu.HBM)
    return pl.pallas_call(functools.partial(force_kernel,J32,JREST,U),
        out_shape=jax.ShapeDtypeStruct((3,CELLS,SLOTS),jnp.float32),
        in_specs=[H]*8,out_specs=V,
        scratch_shapes=[pltpu.VMEM((CELLS,8,SLOTS),jnp.float32),pltpu.VMEM((9,CELLS,SLOTS),jnp.float32),pltpu.VMEM((9,CELLS,SLOTS),jnp.float32),pltpu.SMEM((1,4,128),jnp.int32),pltpu.SMEM((384,),jnp.int32),pltpu.VMEM((MAXT,8,128),jnp.float32),pltpu.SemaphoreType.DMA((6,)),pltpu.VMEM((MAXT,8,128),jnp.float32),pltpu.VMEM((2,144*8,128),jnp.float32),pltpu.VMEM((CELLS,10,SLOTS,128),jnp.float32),pltpu.SemaphoreType.DMA((2,CELLS)),pltpu.VMEM((3,CELLS,SLOTS,128),jnp.float32)],
        compiler_params=pltpu.CompilerParams(vmem_limit_bytes=WHOLE),
        name="force")(rec,snd,rho,meta,tab,buf,cols,rest)


from jax.sharding import PartitionSpec as P

N_GX=16; N_GY=8
AROUND=((-1,-1),(-1,0),(-1,1),(0,-1),(0,1),(1,-1),(1,0),(1,1))
MESH=pl.DeviceIdType.MESH
FAR_FIRST=(6, 10, 7, 9, 2, 14, 5, 11, 8, 3, 13, 1, 15, 4, 12)
OWN_FIELDS=(0, 1, 2, 4, 5, 6, 7)


def neighbours(u, w):
    return [(lax.rem(u + du + N_GX, N_GX), lax.rem(w + dw + N_GY, N_GY)) for du, dw in AROUND]


def exchange_kernel(*refs):
    given, (rec_out, snd_out, meta_out, cols_out), scratch = refs[:8], refs[8:12], refs[12:]
    held, (rec, outbox, inbox, outbox2, inbox2, metas, moved, sounds_moved, cols, load, leave, send1, recv1, send2, recv2) = scratch[:8], scratch[8:]
    pos, vel, mass, smooth, snd, counts, move, lists = held
    u, w = lax.axis_index("gx"), lax.axis_index("gy")
    loads = [pltpu.make_async_copy(src, dst, load.at[k]) for k, (src, dst) in enumerate(zip(given, held))]
    for copy in loads:
        copy.start()
    around = neighbours(u, w)
    barrier = pltpu.get_barrier_semaphore()
    for off in range(1, N_GX):
        pl.semaphore_signal(barrier, inc=1, device_id=(lax.rem(u + off, N_GX), w), device_id_type=MESH)
    for n in (3, 4):
        pl.semaphore_signal(barrier, inc=1, device_id=around[n], device_id_type=MESH)

    for copy in loads:
        copy.wait()
    slot = lax.broadcasted_iota(jnp.int32, (1, 256), 1)
    for c in range(16):
        for f in range(3):
            rec[c, f:f + 1, :] = pos[f, c:c + 1, :]
            rec[c, 5 + f:6 + f, :] = vel[f, c:c + 1, :]
        rec[c, 3:4, :] = jnp.where(slot < counts[c], mass[c:c + 1, :], 0.0)
        rec[c, 4:5, :] = smooth[c:c + 1, :]

    headed = [lax.shift_right_logical(move[c], 7) for c in range(16)]
    row = lax.broadcasted_iota(jnp.int32, (8, 256), 0)

    def post(off, _):
        column = lax.rem(u + off, N_GX)
        first, last = jnp.int32(16), jnp.int32(-1)
        for c in range(16):
            match = headed[c] == column
            first = jnp.minimum(first, jnp.where(match, c, 16))
            last = jnp.where(match, c, last)
        found = last >= 0
        first = jnp.where(found, first, 0)
        last = jnp.where(found, last, 0)
        outbox[off, 0:8, :] = rec[first]
        outbox2[off] = rec[last]
        number = lambda c: jnp.where(found, move[c], -1).astype(jnp.float32)
        amount = lambda c: counts[c].astype(jnp.float32)
        more = jnp.where(row == 0, snd[pl.ds(first, 1), :], snd[pl.ds(last, 1), :])
        more = jnp.where(row == 2, number(first), more)
        more = jnp.where(row == 3, number(last), more)
        more = jnp.where(row == 4, amount(first), more)
        more = jnp.where(row == 5, amount(last), more)
        outbox[off, 8:16, :] = more
        return 0

    lax.fori_loop(0, N_GX, post, 0)
    pl.semaphore_wait(barrier, N_GX - 1 + 2)

    def parcel(off, part):
        src, dst = ((outbox, inbox), (outbox2, inbox2))[part]
        return pltpu.make_async_remote_copy(
            src_ref=src.at[off], dst_ref=dst.at[off], send_sem=send1.at[part, off], recv_sem=recv1.at[part, off],
            device_id=(lax.rem(u + off, N_GX), w), device_id_type=MESH)

    for part in range(2):
        for off in FAR_FIRST:
            parcel(off, part).start()
    inbox[0] = outbox[0]
    inbox2[0] = outbox2[0]

    first_own = ((u * N_GY + w) * 16).astype(jnp.float32)
    sub = lax.broadcasted_iota(jnp.int32, (16, 256), 0).astype(jnp.float32) + first_own
    lane = lax.broadcasted_iota(jnp.int32, (1, 128), 1).astype(jnp.float32) + first_own

    def place(cells, block, number, rank):
        key = jnp.broadcast_to(jnp.where(number >= 0.0, rank, -1.0), (8, 256))
        cells = tuple(jnp.where(key == float(k), block, cells[k]) for k in range(8))
        return cells, rank + jnp.where(number >= 0.0, 1.0, 0.0)

    def absorb(off, carry):
        cells, rank, sounds, amounts, ranks = carry
        for k in range(2):
            number = inbox[off, 10 + k:11 + k, :]
            mine = lane == number[:, 0:128]
            sounds = jnp.where(sub == number, inbox[off, 8 + k:9 + k, :], sounds)
            amounts = jnp.where(mine, inbox[off, 12 + k:13 + k, 0:128], amounts)
            ranks = jnp.where(mine, rank[:, 0:128] + 8.0 * k, ranks)
        cells, rank = place(cells, inbox[off, 0:8, :], inbox[off, 10:11, :], rank)
        return cells, rank, sounds, amounts, ranks

    def absorb_next(off, carry):
        parcel(off, 0).wait_recv()
        return absorb(off, carry)

    def absorb2(off, carry):
        return place(carry[0], inbox2[off], inbox[off, 10:11, :], carry[1])

    def absorb2_next(off, carry):
        parcel(off, 1).wait_recv()
        return absorb2(off, carry)

    zero = jnp.zeros((8, 256), jnp.float32)
    line = jnp.zeros((1, 128), jnp.float32)
    none = ((zero,) * 8, jnp.zeros((1, 256), jnp.float32))
    carry = absorb(0, none + (jnp.zeros((16, 256), jnp.float32), line, line))
    cells, _, sounds, amounts, ranks = lax.fori_loop(1, N_GX, absorb_next, carry)
    for k in range(8):
        moved[k] = cells[k]
    sounds_moved[...] = sounds
    metas[0:1, :] = amounts.astype(jnp.int32)
    metas[1:2, :] = lists[...]
    metas[2:3, :] = ranks.astype(jnp.int32)
    metas[3:4, :] = lists[...]

    halves = (pl.ds(0, 8), pl.ds(8, 8))
    own = (metas, moved.at[halves[0]], sounds_moved, moved.at[halves[1]])
    at = lambda n: (meta_out.at[n], rec_out.at[n, halves[0]], snd_out.at[n], rec_out.at[n, halves[1]])
    remote = lambda src, n, k, device: pltpu.make_async_remote_copy(
        src_ref=src, dst_ref=at(n + 1)[k], send_sem=send2.at[n, k], recv_sem=recv2.at[n, k],
        device_id=device, device_id_type=MESH)
    copies, arriving = [], {}

    def spread_out(items):
        for nearest in ((1, 6), (3, 4)):
            for k in items:
                for n in nearest:
                    copy = remote(own[k], n, k, around[n])
                    copy.start()
                    if nearest == (1, 6):
                        arriving[n, k] = copy
                    else:
                        copies.append(copy)

    def pass_on(items):
        for k in items:
            for n in (1, 6):
                arriving[n, k].wait_recv()
                for to, step in ((n - 1, 3), (n + 1, 4)):
                    copy = remote(at(n + 1)[k], to, k, around[step])
                    copy.start()
                    copies.append(copy)

    def column_copy(k):
        return pltpu.make_async_copy(cols.at[k], cols_out.at[k], leave.at[k])

    def make_columns(k, _):
        columns(cols.at[k], moved[k], OWN_FIELDS)
        column_copy(k).start()
        return 0

    spread_out((0, 1, 2))
    cells, _ = lax.fori_loop(1, N_GX, absorb2_next, absorb2(0, none))
    for k in range(8):
        moved[8 + k] = cells[k]
    spread_out((3,))
    for k in range(4):
        copy = pltpu.make_async_copy(own[k], at(0)[k], load.at[k])
        copy.start()
        copies.append(copy)
    pass_on((0, 1, 2, 3))
    lax.fori_loop(0, 16, make_columns, 0)
    for copy in arriving.values():
        copy.wait_send()

    def left(k, _):
        column_copy(k).wait()
        return 0

    lax.fori_loop(0, 16, left, 0)

    def sent(off, _):
        parcel(off, 0).wait_send()
        parcel(off, 1).wait_send()
        return 0

    lax.fori_loop(1, N_GX, sent, 0)
    for copy in copies:
        copy.wait()


VMEM=pl.BlockSpec(memory_space=pltpu.VMEM)
HBM=pl.BlockSpec(memory_space=pltpu.HBM)

def exchange(positions, velocities, masses, smoothing, sound2, counts, move_to, lists):
    return pl.pallas_call(
        exchange_kernel,
        out_shape=(jax.ShapeDtypeStruct((9, 16, 8, 256), jnp.float32),
                   jax.ShapeDtypeStruct((9, 16, 256), jnp.float32),
                   jax.ShapeDtypeStruct((9, 4, 128), jnp.int32),
                   jax.ShapeDtypeStruct((16, 7, 256, 128), jnp.float32)),
        in_specs=[HBM] * 8,
        out_specs=(HBM,) * 4,
        scratch_shapes=[
            pltpu.VMEM((3, 16, 256), jnp.float32),
            pltpu.VMEM((3, 16, 256), jnp.float32),
            pltpu.VMEM((16, 256), jnp.float32),
            pltpu.VMEM((16, 256), jnp.float32),
            pltpu.VMEM((16, 256), jnp.float32),
            pltpu.SMEM((16,), jnp.int32),
            pltpu.SMEM((16,), jnp.int32),
            pltpu.VMEM((1, 128), jnp.int32),
            pltpu.VMEM((16, 8, 256), jnp.float32),
            pltpu.VMEM((N_GX, 16, 256), jnp.float32),
            pltpu.VMEM((N_GX, 16, 256), jnp.float32),
            pltpu.VMEM((N_GX, 8, 256), jnp.float32),
            pltpu.VMEM((N_GX, 8, 256), jnp.float32),
            pltpu.VMEM((4, 128), jnp.int32),
            pltpu.VMEM((16, 8, 256), jnp.float32),
            pltpu.VMEM((16, 256), jnp.float32),
            pltpu.VMEM((16, 7, 256, 128), jnp.float32),
            pltpu.SemaphoreType.DMA((8,)),
            pltpu.SemaphoreType.DMA((16,)),
            pltpu.SemaphoreType.DMA((2, N_GX)),
            pltpu.SemaphoreType.DMA((2, N_GX)),
            pltpu.SemaphoreType.DMA((8, 4)),
            pltpu.SemaphoreType.DMA((8, 4)),
        ],
        compiler_params=pltpu.CompilerParams(collective_id=0, has_side_effects=True, vmem_limit_bytes=WHOLE),
        name="exchange",
    )(positions, velocities, masses, smoothing, sound2, counts, move_to, lists)


def share_kernel(own, snd, out, rest_out, own_here, snd_here, rest, load, leave, send, recv):
    u, w = lax.axis_index("gx"), lax.axis_index("gy")
    around = neighbours(u, w)
    barrier = pltpu.get_barrier_semaphore()
    for n in range(8):
        pl.semaphore_signal(barrier, inc=1, device_id=around[n], device_id_type=MESH)
    loads = [pltpu.make_async_copy(own, own_here, load.at[0]), pltpu.make_async_copy(snd.at[0], snd_here, load.at[1])]
    copies = [pltpu.make_async_copy(own, out.at[0], load.at[2])]
    for copy in loads + copies:
        copy.start()
    for copy in loads:
        copy.wait()
    pl.semaphore_wait(barrier, 8)
    for n in range(8):
        copy = pltpu.make_async_remote_copy(
            src_ref=own_here, dst_ref=out.at[n + 1], send_sem=send.at[n], recv_sem=recv.at[n],
            device_id=around[n], device_id_type=MESH)
        copy.start()
        copies.append(copy)
    fields = extra_fields(snd_here[...], own_here[...])
    for a in range(16):
        columns(rest.at[a], jnp.concatenate([field[a:a + 1] for field in fields], 0), (0, 1, 2))
        copy = pltpu.make_async_copy(rest.at[a], rest_out.at[a], leave.at[a])
        copy.start()
        copies.append(copy)
    for copy in copies:
        copy.wait()


def share(own, snd):
    return pl.pallas_call(
        share_kernel,
        out_shape=(jax.ShapeDtypeStruct((9, 16, 256), jnp.float32), jax.ShapeDtypeStruct((16, 3, 256, 128), jnp.float32)),
        in_specs=[HBM] * 2, out_specs=(HBM,) * 2,
        scratch_shapes=[
            pltpu.VMEM((16, 256), jnp.float32),
            pltpu.VMEM((16, 256), jnp.float32),
            pltpu.VMEM((16, 3, 256, 128), jnp.float32),
            pltpu.SemaphoreType.DMA((3,)),
            pltpu.SemaphoreType.DMA((16,)),
            pltpu.SemaphoreType.DMA((8,)),
            pltpu.SemaphoreType.DMA((8,)),
        ],
        compiler_params=pltpu.CompilerParams(collective_id=1, has_side_effects=True, vmem_limit_bytes=WHOLE),
        name="share",
    )(own, snd)


def body(positions, velocities, masses, smoothing, sound2, counts, move_to, proxy_send, pairs):
    rec, snd, meta, cols = exchange(positions, velocities, masses, smoothing, sound2, counts, move_to, proxy_send.reshape(1, 128))
    rec = rec.reshape(144, 8, 256)
    rho, safe, tab, buf = density(rec, meta, pairs.T, cols)
    rho_all, rest = share(safe, snd)
    accel = force(rec, snd, rho_all, meta, tab, buf, cols, rest)
    return rho, accel


def solution(mesh):
    flat, cells, three = P(("gx", "gy")), P(("gx", "gy"), None), P(None, ("gx", "gy"), None)
    return jax.shard_map(
        body, mesh=mesh,
        in_specs=(three, three, cells, cells, cells, flat, flat, flat, cells),
        out_specs=(cells, three), check_vma=False)
```
